32 devices in a mesh: groups: 2 (over y), dp: 4 (over x, core), tensor: 4 (over z).
Axes of the slice: x: 2, y: 2, z: 4, core: 2. Of those that a mesh axis runs over, the one named last changes fastest.
Arguments:
- row_adapter_index: int32 [192], P(('groups', 'dp')), parts along dimension 0, may hold values from 0 to 63
- adapter_storage_row: int32 [64], replicated, may hold values from 0 to 63, each once
- initial_head_state: bfloat16 [192, 128, 64, 128], P(('groups', 'dp'), 'tensor'), parts along dimension 0, may hold values from -0.59765625 to 0.59765625
- step_head_input: bfloat16 [4, 192, 8192], P(None, ('groups', 'dp'), 'tensor'), parts along dimension 1, may hold values from -20 to 20
- step_gate_input: bfloat16 [4, 192, 8192], P(None, ('groups', 'dp'), 'tensor'), parts along dimension 1, may hold values from -6 to 6
- step_size_logits: float32 [4, 192, 128], P(None, ('groups', 'dp'), 'tensor'), parts along dimension 1, may hold values from -6 to 6
- state_write_key: bfloat16 [4, 192, 128], P(None, ('groups', 'dp')), parts along dimension 1, may hold values from -0.5 to 0.5
- state_read_query: bfloat16 [4, 192, 128], P(None, ('groups', 'dp')), parts along dimension 1, may hold values from -6 to 6
- head_decay_rate: float32 [128], P('tensor'), may hold values from 0.03 to 3
- head_skip_gain: float32 [128], P('tensor'), may hold values from 0.5 to 1.5
- gated_norm_gain: float32 [8192], P('tensor'), may hold values from 0.1 to 1.9
- output_weight: bfloat16 [8192, 4096], P('tensor'), may hold values from -0.0625 to 0.0625
- adapter_down_weight: bfloat16 [64, 8192, 64], P('dp', 'tensor'), may hold values from -0.0625 to 0.0625
- adapter_up_weight: bfloat16 [64, 64, 4096], P('dp', None, 'tensor'), may hold values from -0.75 to 0.75
Outputs:
- mixed_out: bfloat16 [4, 192, 4096], P(None, ('groups', 'dp'), 'tensor'), parts along dimension 1
- new_state: bfloat16 [192, 128, 64, 128], P(('groups', 'dp'), 'tensor'), parts along dimension 0
The draws below stay inside these ranges and needn't reach their ends.
There are 2 independent parts, one for each index of `groups`. The reference program is written for one: setup_inputs(seed, part) draws one part's arguments, and reference() takes and returns one part's arrays. A program takes and returns all parts, laid end to end along the dimension named above; an argument that names none is the same for every part. Nothing has to cross between parts.
Inputs may be any that keep to these rules, and one draw needn't show every extreme that they name: Row r uses the adapter row_adapter_index[r]. A permutation: adapter a is stored in row adapter_storage_row[a] of adapter_down_weight and adapter_up_weight.
All inputs are finite; a program needn't handle non-finite values.
Results may differ from the reference program's by a relative error of at most 0.009.
Values may be sent and summed in bfloat16 or wider, within the bound.
No kernel may reach another device: no remote copies, remote signals or barrier semaphores. Data moves between devices by JAX's collectives and lax.ppermute only.
A program may use at most 128 MiB of HBM per device.

```python
import math
import jax
import jax.numpy as jnp
import numpy as np
from jax import lax

MODEL_WIDTH = 4096
STATE_HEADS = 128
HEAD_WIDTH = 64
N = 128
ADAPTER_RANK = 64
STEPS = 4
ROWS = 96
ADAPTER_TOTAL = 64


def draw_step_head_input(key, part):
    key = jax.random.fold_in(key, 7)
    first, second = jax.random.split(key)
    width = STATE_HEADS * HEAD_WIDTH
    column = jnp.arange(width, dtype=jnp.float32) / (width - 1)
    rough = jnp.exp(jax.random.uniform(second, (width,), jnp.float32, -0.7, 0.7))
    noise = jnp.clip(jax.random.normal(first, (STEPS, ROWS, width), jnp.float32), -4.0, 4.0)
    ramp = jnp.exp(1.1 * column)
    return (noise * ramp[None, None, :] * rough[None, None, :] * 0.6).astype(jnp.bfloat16)


def set_ends(drawn, key, least, top_value):
    extent = drawn.shape
    index_at = [jax.random.randint(jax.random.fold_in(key, axis), (), 0, extent[axis]) for axis in range(len(extent))]
    drawn = drawn.at[tuple(index_at)].set(least)
    longest = extent.index(max(extent))
    index_at[longest] = (index_at[longest] + 1) % extent[longest]
    return drawn.at[tuple(index_at)].set(top_value)


def level_of(rng, extent, cuts, low, high):
    def one(position, blocks):
        heights = jax.random.uniform(jax.random.fold_in(jax.random.fold_in(rng, 6), position), (blocks,), jnp.float32, low / len(cuts), high / len(cuts))
        return jnp.repeat(jnp.exp(heights), extent[position] // blocks).reshape((-1,) + (1,) * (len(extent) - position - 1))

    level = one(*cuts[0])
    for cut in cuts[1:]:
        level = level * one(*cut)
    return level


def cumulative_ranks(number_of, lean):
    loads = [(1 << 20) // math.isqrt(standing ** lean) + 1 for standing in range(1, number_of + 1)]
    spread = 1 + sum(loads) // (1 << 30)
    return np.cumsum(np.array([max(1, weight // spread) for weight in loads]))


def ranked_ids(rng, extent, number_of, lean):
    grid = cumulative_ranks(number_of, lean)
    ticket = jax.random.randint(jax.random.fold_in(rng, 1), extent, 0, int(grid[number_of - 1]))
    standing = jnp.searchsorted(jnp.asarray(grid, jnp.int32), ticket, side="right")
    return jax.random.permutation(jax.random.fold_in(rng, 2), number_of)[standing].astype(jnp.int32)


def scatter_about(own_key, dims, scale, reach, cuts=(), kind=jnp.bfloat16):
    factor_of = level_of(own_key, dims, cuts, -0.22, 0.18) if cuts else 1.0
    result = jax.random.normal(own_key, dims, jnp.float32) * scale * factor_of
    return jnp.minimum(jnp.maximum(result, -reach), reach).astype(kind)


def setup_inputs(seed: int = 0, part: int = 0) -> dict:
    key_list = jax.random.split(jax.random.key(seed), 15)
    part_splits = jax.random.split(jax.random.fold_in(key_list[14], part), 15)
    return {
        "row_adapter_index": set_ends(ranked_ids(part_splits[0], (ROWS,), ADAPTER_TOTAL, 2), jax.random.fold_in(part_splits[0], 3), 0, ADAPTER_TOTAL - 1).astype(jnp.int32),
        "adapter_storage_row": jax.random.permutation(key_list[1], ADAPTER_TOTAL).astype(jnp.int32),
        "initial_head_state": scatter_about(part_splits[2], (ROWS, STATE_HEADS, HEAD_WIDTH, N), 0.1, 0.59765625, ((0, 4), (1, 4))),
        "step_head_input": draw_step_head_input(jax.random.fold_in(jax.random.fold_in(key_list[14], part), 71), part),
        "step_gate_input": scatter_about(part_splits[4], (STEPS, ROWS, STATE_HEADS * HEAD_WIDTH), 1.0, 6.0, ((1, 4), (2, 4))),
        "step_size_logits": scatter_about(part_splits[5], (STEPS, ROWS, STATE_HEADS), 1.0, 6.0, ((1, 4), (2, 4)), jnp.float32),
        "state_write_key": scatter_about(part_splits[6], (STEPS, ROWS, N), N ** -0.5, 0.5, ((1, 4),)),
        "state_read_query": scatter_about(part_splits[7], (STEPS, ROWS, N), 1.0, 6.0, ((1, 4),)),
        "head_decay_rate": jnp.clip(jnp.exp(math.log(3.0) - 4.6051702 * jax.random.uniform(key_list[8], (STATE_HEADS,), jnp.float32) ** level_of(key_list[8], (STATE_HEADS,), ((0, 4),), -0.2, 0.2)), 0.03, 3.0),
        "head_skip_gain": jnp.clip(0.5 + 1.0 * jax.random.uniform(key_list[9], (STATE_HEADS,), jnp.float32) ** level_of(key_list[9], (STATE_HEADS,), ((0, 4),), -0.2, 0.2), 0.5, 1.5),
        "gated_norm_gain": jnp.clip(1.0 + 0.18 * jax.random.normal(key_list[10], (STATE_HEADS * HEAD_WIDTH,), jnp.float32), 0.1, 1.9),
        "output_weight": scatter_about(key_list[11], (STATE_HEADS * HEAD_WIDTH, MODEL_WIDTH), (STATE_HEADS * HEAD_WIDTH) ** -0.5, 0.0625, ((0, 4),)),
        "adapter_down_weight": scatter_about(key_list[12], (ADAPTER_TOTAL, STATE_HEADS * HEAD_WIDTH, ADAPTER_RANK), (STATE_HEADS * HEAD_WIDTH) ** -0.5, 0.0625, ((0, 4), (1, 4))),
        "adapter_up_weight": scatter_about(key_list[13], (ADAPTER_TOTAL, ADAPTER_RANK, MODEL_WIDTH), ADAPTER_RANK ** -0.5, 0.75, ((0, 4), (2, 4))),
    }


EPSILON = 1e-05

def advance(initial_head_state, step_head_input, step_gate_input, step_size_logits, state_write_key, state_read_query, head_decay_rate, head_skip_gain, gated_norm_gain):
    row_count = initial_head_state.shape[0]
    head_count = initial_head_state.shape[1]
    head_dim = initial_head_state.shape[2]
    carried = initial_head_state
    normed_all = []
    for moment in range(step_head_input.shape[0]):
        delta_t = jax.nn.softplus(step_size_logits[moment].astype(jnp.float32))
        damping = jnp.exp(-delta_t * head_decay_rate[None, :])
        values = step_head_input[moment].astype(jnp.float32).reshape(row_count, head_count, head_dim)
        writer = state_write_key[moment].astype(jnp.float32)
        reader = state_read_query[moment].astype(jnp.float32)
        updated = damping[:, :, None, None] * carried.astype(jnp.float32) + (delta_t[:, :, None] * values)[:, :, :, None] * writer[:, None, None, :]
        carried = updated.astype(jnp.bfloat16)
        output = lax.optimization_barrier(jnp.sum(updated * reader[:, None, None, :], axis=3)) + head_skip_gain[None, :, None] * values
        gated_out = output.reshape(row_count, head_count * head_dim) * jax.nn.silu(step_gate_input[moment].astype(jnp.float32))
        mean_sq = lax.optimization_barrier(jnp.mean(gated_out * gated_out, axis=1, keepdims=True))
        normed_all.append((gated_out * lax.rsqrt(mean_sq + EPSILON) * gated_norm_gain[None, :]).astype(jnp.bfloat16))
    return (jnp.stack(normed_all), carried)

def reference(row_adapter_index, adapter_storage_row, initial_head_state, step_head_input, step_gate_input, step_size_logits, state_write_key, state_read_query, head_decay_rate, head_skip_gain, gated_norm_gain, output_weight, adapter_down_weight, adapter_up_weight):
    normed, carried = advance(initial_head_state, step_head_input, step_gate_input, step_size_logits, state_write_key, state_read_query, head_decay_rate, head_skip_gain, gated_norm_gain)
    steps_n, row_count, width = normed.shape
    flat = normed.reshape(steps_n * row_count, width)
    base = jnp.dot(flat, output_weight, preferred_element_type=jnp.float32).reshape(steps_n, row_count, -1)
    slots = adapter_storage_row[row_adapter_index].astype(jnp.int32)

    def per_row(pair):
        normed_row_output, storage_row_index = pair
        down_projected = jnp.dot(normed_row_output, adapter_down_weight[storage_row_index], preferred_element_type=jnp.float32).astype(jnp.bfloat16)
        return jnp.dot(down_projected, adapter_up_weight[storage_row_index], preferred_element_type=jnp.float32)
    deltas = lax.map(per_row, (jnp.swapaxes(normed, 0, 1), slots))
    mixed_out = (base + jnp.swapaxes(deltas, 0, 1)).astype(jnp.bfloat16)
    return (mixed_out, carried)
```

```python
import functools

import jax
import jax.numpy as jnp
from jax import lax
from jax.experimental import pallas as pl
from jax.experimental.pallas import tpu as pltpu
from jax.sharding import PartitionSpec as P

STATE_HEADS = 128
HEAD_WIDTH = 64
EPSILON = 1e-05

BF = jnp.bfloat16
F32 = jnp.float32
NT = (((1,), (1,)), ((), ()))
TN = (((0,), (0,)), ((), ()))
NN = (((1,), (0,)), ((), ()))
LANES = 128
EXT = 16


def dot(a, b, dims=NN):
    return lax.dot_general(a, b, dims, preferred_element_type=F32)


def state_body(
    first_block, with_slots, hb, steps, rows, heads, *refs
):
    refs = list(refs)
    if with_slots:
        idx_ref, store_ref = refs.pop(0), refs.pop(0)
    (x_ref, g_ref, lg_ref, rate_ref, skip_ref, gain_ref, w_ref, q_ref, s_ref) = refs[:9]
    refs = refs[9:]
    if not with_slots:
        refs = refs[1:]
    ns_ref, u_ref, ss_ref = refs[:3]
    chi_ref, clo_ref, wbd_ref, qbd_ref, k4_ref, slot_ref = refs[3:]
    j = pl.program_id(0)
    tr = steps * rows
    cols = hb * HEAD_WIDTH
    n = w_ref.shape[2]
    pairs = rows // 2

    @pl.when(j == 0)
    def _():
        delta = [jax.nn.softplus(lg_ref[t]) for t in range(steps)]
        keep = [jnp.exp(-delta[t] * rate_ref[...]) for t in range(steps)]
        w = [w_ref[t].astype(F32) for t in range(steps)]
        q = [q_ref[t].astype(F32) for t in range(steps)]
        cum = []
        for t in range(steps):
            cum.append(keep[t] if t == 0 else cum[-1] * keep[t])
        c = [delta[s] for s in range(steps)]
        coef = list(cum)
        cur = []
        for t in range(steps):
            cur = [v * keep[t] for v in cur] + [delta[t]]
            for s in range(t + 1):
                dotted = jnp.sum(w[s] * q[t], axis=1, keepdims=True)
                a = cur[s] * dotted
                if s == t:
                    a = a + skip_ref[...]
                coef.append(a)
        coef += cur
        coef = jnp.concatenate(coef, axis=0)
        hi = coef.astype(BF)
        chi_ref[...] = hi
        clo_ref[...] = (coef - hi.astype(F32)).astype(BF)
        eye = lax.broadcasted_iota(jnp.int32, (heads, heads), 0) == lax.broadcasted_iota(
            jnp.int32, (heads, heads), 1
        )
        for r in range(rows):
            col = jnp.sum(jnp.where(eye, cum[-1][r : r + 1, :], 0.0), axis=1, keepdims=True)
            k4_ref[r] = jnp.broadcast_to(col, (heads, LANES))
        wf = jnp.concatenate(w, axis=0)
        qf = jnp.concatenate(q, axis=0)
        owner = lax.rem(lax.broadcasted_iota(jnp.int32, (tr, n), 0), rows)
        for p in range(pairs):
            for half in range(2):
                mine = owner == 2 * p + half
                wbd_ref[p, :, half * n : (half + 1) * n] = jnp.where(mine, wf, 0.0).astype(BF)
                qbd_ref[p, :, half * n : (half + 1) * n] = jnp.where(mine, qf, 0.0).astype(BF)
        ss_ref[...] = jnp.zeros_like(ss_ref)
        if with_slots:
            for r in range(rows):
                slot = store_ref[idx_ref[r]].astype(F32)
                for t in range(steps):
                    slot_ref[t * rows + r : t * rows + r + 1, :] = jnp.full((1, LANES), slot, F32)
            for b in range(u_ref.shape[1] // LANES):
                lo = min(b * EXT, tr - EXT)
                u_ref[tr : tr + EXT, b * LANES : (b + 1) * LANES] = slot_ref[lo : lo + EXT, :].astype(BF)

    block = first_block + j
    hsel = lax.broadcasted_iota(jnp.int32, (heads, cols), 0)
    hcol = lax.broadcasted_iota(jnp.int32, (heads, cols), 1) // HEAD_WIDTH + block * hb
    expand = jnp.where(hsel == hcol, 1.0, 0.0).astype(BF)
    ce = dot(chi_ref[...], expand) + dot(clo_ref[...], expand)
    x = [x_ref[t].astype(F32) for t in range(steps)]
    last = ce.shape[0] - tr
    xe = jnp.concatenate(
        [ce[last + s * rows : last + (s + 1) * rows] * x[s] for s in range(steps)], axis=0
    )
    xet = xe.T.astype(BF)
    z = jnp.zeros((tr, cols), F32)
    for p in range(pairs):
        s0 = s_ref[2 * p].reshape(cols, n)
        s1 = s_ref[2 * p + 1].reshape(cols, n)
        z = z + dot(qbd_ref[p], jnp.concatenate([s0, s1], axis=1), NT)
        up = dot(xet, wbd_ref[p])
        for half, sv in ((0, s0), (1, s1)):
            r = 2 * p + half
            k4 = k4_ref[r, pl.ds(block * hb, hb), :]
            grown = (
                k4[:, None, :] * sv.astype(F32).reshape(hb, HEAD_WIDTH, n)
                + up[:, half * n : (half + 1) * n].reshape(hb, HEAD_WIDTH, n)
            )
            ns_ref[r] = grown.astype(BF)
    gain = gain_ref[...]
    at = tr
    out_rows = []
    for t in range(steps):
        y = ce[t * rows : (t + 1) * rows] * z[t * rows : (t + 1) * rows]
        for s in range(t + 1):
            y = y + ce[at : at + rows] * x[s]
            at += rows
        g = g_ref[t].astype(F32)
        gated = y * (g / (1.0 + jnp.exp(-g)))
        sq = gated * gated
        part = sq[:, :LANES]
        for b in range(1, cols // LANES):
            part = part + sq[:, b * LANES : (b + 1) * LANES]
        ss_ref[t * rows : (t + 1) * rows, :] += part
        out_rows.append(gated * gain)
    u_ref[:tr, pl.ds(pl.multiple_of(j * cols, cols), cols)] = jnp.concatenate(out_rows, axis=0).astype(BF)


def state_call(args, part, parts, hb, carried=None):
    (idx, store, state, x, g, lg, w, q, rate, skip, gain) = args
    steps, rows, width = x.shape
    heads = rate.shape[0]
    tr = steps * rows
    cols = hb * HEAD_WIDTH
    n = w.shape[2]
    grid = heads // hb // parts
    first = part * grid
    with_slots = part == 0
    blocked = lambda j: (0, 0, first + j)
    whole3 = lambda j: (0, 0, 0)
    whole2 = lambda j: (0, 0)
    state_spec = pl.BlockSpec((rows, hb, HEAD_WIDTH, n), lambda j: (0, first + j, 0, 0))
    in_specs = [
        pl.BlockSpec((steps, rows, cols), blocked),
        pl.BlockSpec((steps, rows, cols), blocked),
        pl.BlockSpec((steps, rows, heads), whole3),
        pl.BlockSpec((1, heads), whole2),
        pl.BlockSpec((1, heads), whole2),
        pl.BlockSpec((1, cols), lambda j: (0, first + j)),
        pl.BlockSpec((steps, rows, n), whole3),
        pl.BlockSpec((steps, rows, n), whole3),
        state_spec,
    ]
    operands = [x, g, lg, rate[None], skip[None], gain[None], w, q, state]
    aliases = {}
    if with_slots:
        in_specs = [pl.BlockSpec(memory_space=pltpu.SMEM)] * 2 + in_specs
        operands = [idx, store] + operands
    else:
        in_specs.append(pl.BlockSpec(memory_space=pl.ANY))
        operands.append(carried)
        aliases = {len(operands) - 1: 0}
    u_rows = tr + (EXT if with_slots else 0)
    u_cols = width // parts
    coef_rows = (steps * (steps + 1) // 2 + 2 * steps) * rows
    return pl.pallas_call(
        functools.partial(state_body, first, with_slots, hb, steps, rows, heads),
        grid=(grid,),
        in_specs=in_specs,
        out_specs=[
            state_spec,
            pl.BlockSpec((u_rows, u_cols), whole2),
            pl.BlockSpec((tr, LANES), whole2),
        ],
        out_shape=[
            jax.ShapeDtypeStruct(state.shape, BF),
            jax.ShapeDtypeStruct((u_rows, u_cols), BF),
            jax.ShapeDtypeStruct((tr, LANES), F32),
        ],
        scratch_shapes=[
            pltpu.VMEM((coef_rows, heads), BF),
            pltpu.VMEM((coef_rows, heads), BF),
            pltpu.VMEM((rows // 2, tr, 2 * n), BF),
            pltpu.VMEM((rows // 2, tr, 2 * n), BF),
            pltpu.VMEM((rows, heads, LANES), F32),
            pltpu.VMEM((tr, LANES), F32),
        ],
        input_output_aliases=aliases,
        compiler_params=pltpu.CompilerParams(
            dimension_semantics=("arbitrary",), vmem_limit_bytes=40 * 1024 * 1024
        ),
        cost_estimate=pl.CostEstimate(
            flops=4 * tr * rows * heads * HEAD_WIDTH * n // parts,
            bytes_accessed=4 * state.size // parts,
            transcendentals=0,
        ),
        name=f"state_part{part}",
    )(*operands)


def base_body(per, count, order_ref, u1_ref, u2_ref, w_ref, *outs):
    tr, half = u2_ref.shape
    tile = dot(u1_ref[:tr], w_ref[:half]) + dot(u2_ref[...], w_ref[half:])
    step = pl.program_id(0)
    for k in range(count):

        @pl.when(step // per == k)
        def _():
            outs[k][...] = tile.astype(outs[k].dtype)


def base_call(u1, u2, weight, order, features, types, tile, name):
    tr = u2.shape[0]
    count = len(types)
    per = features // tile
    depth = weight.shape[0]

    def out_map(k):
        return lambda g, o: (0, jnp.clip(g - k * per, 0, per - 1))

    return pl.pallas_call(
        functools.partial(base_body, per, count),
        grid_spec=pltpu.PrefetchScalarGridSpec(
            num_scalar_prefetch=1,
            grid=(count * per,),
            in_specs=[
                pl.BlockSpec(u1.shape, lambda g, o: (0, 0)),
                pl.BlockSpec(u2.shape, lambda g, o: (0, 0)),
                pl.BlockSpec((depth, tile), lambda g, o: (0, o[g // per] * per + g % per)),
            ],
            out_specs=[pl.BlockSpec((tr, tile), out_map(k)) for k in range(count)],
        ),
        out_shape=[jax.ShapeDtypeStruct((tr, features), t) for t in types],
        compiler_params=pltpu.CompilerParams(
            dimension_semantics=("arbitrary",), vmem_limit_bytes=24 * 1024 * 1024
        ),
        cost_estimate=pl.CostEstimate(
            flops=2 * tr * depth * features * count,
            bytes_accessed=2 * depth * features * count,
            transcendentals=0,
        ),
        name=name,
    )(order, u1, u2, weight)


def slot_column(u1_ref, tr):
    blocks = [u1_ref[tr : tr + EXT, b * LANES : b * LANES + LANES].astype(F32) for b in range(tr // EXT)]
    return jnp.concatenate(blocks, axis=0)


def down_body(sources, rank, *refs):
    first_ref = refs[0]
    u1s = refs[1 : 1 + sources]
    u2s = refs[1 + sources : 1 + 2 * sources]
    down_ref, ssa_ref, ssb_ref, msg_ref, acc_ref = refs[1 + 2 * sources :]
    tr, half = u2s[0].shape
    g = pl.program_id(0)
    tile = down_ref.shape[0]
    base = first_ref[0] + g * (tile // rank)
    cell = (lax.broadcasted_iota(jnp.int32, (tr, tile), 1) // rank + base).astype(F32)
    for k in range(sources):
        part = dot(u1s[k][:tr], down_ref[:, :half], NT) + dot(u2s[k][...], down_ref[:, half:], NT)
        slot = slot_column(u1s[k], tr)
        slot = jnp.concatenate([slot] * (tile // LANES), axis=1)
        part = jnp.where(cell == slot, part, 0.0)
        total = part[:, :LANES]
        for b in range(1, tile // LANES):
            total = total + part[:, b * LANES : (b + 1) * LANES]

        @pl.when(g == 0)
        def _():
            acc_ref[k] = total

        @pl.when(g > 0)
        def _():
            acc_ref[k] += total

    @pl.when(g == pl.num_programs(0) - 1)
    def _():
        lane = lax.broadcasted_iota(jnp.int32, (tr, LANES), 1)
        for k in range(0, sources, 2):
            a, b = acc_ref[k], acc_ref[k + 1]
            a = a + pltpu.roll(a, rank, 1)
            b = b + pltpu.roll(b, rank, 1)
            at = k // 2 * tr
            msg_ref[at : at + tr, :] = jnp.where(lane < rank, a, b).astype(BF)
        ss = jnp.sum(ssa_ref[...] + ssb_ref[...], axis=1, keepdims=True)
        ss = jnp.broadcast_to(ss, (tr, LANES))
        hi = ss.astype(BF).astype(F32)
        lo = ss - hi
        lane = lax.broadcasted_iota(jnp.int32, (EXT, LANES), 1)
        row = jnp.zeros((EXT, LANES), F32)
        for b in range(tr // EXT):
            piece = slice(b * EXT, (b + 1) * EXT)
            row = jnp.where(lane == 2 * b, hi[piece], row)
            row = jnp.where(lane == 2 * b + 1, lo[piece], row)
        msg_ref[sources // 2 * tr :, :] = row.astype(BF)


def down_call(first, u1s, u2s, down, rank, ssa, ssb, tile=256):
    tr = u2s[0].shape[0]
    sources = len(u1s)
    wide, depth = down.shape
    whole = lambda a: pl.BlockSpec(a.shape, lambda g: (0, 0))
    return pl.pallas_call(
        functools.partial(down_body, sources, rank),
        grid=(wide // tile,),
        in_specs=[pl.BlockSpec(memory_space=pltpu.SMEM)]
        + [whole(a) for a in u1s]
        + [whole(a) for a in u2s]
        + [pl.BlockSpec((tile, depth), lambda g: (g, 0)), whole(ssa), whole(ssb)],
        out_specs=pl.BlockSpec((sources // 2 * tr + EXT, LANES), lambda g: (0, 0)),
        out_shape=jax.ShapeDtypeStruct((sources // 2 * tr + EXT, LANES), BF),
        scratch_shapes=[pltpu.VMEM((sources, tr, LANES), F32)],
        compiler_params=pltpu.CompilerParams(
            dimension_semantics=("arbitrary",), vmem_limit_bytes=24 * 1024 * 1024
        ),
        cost_estimate=pl.CostEstimate(
            flops=2 * sources * tr * wide * depth, bytes_accessed=2 * wide * depth, transcendentals=0
        ),
        name="adapter_down",
    )(first, *u1s, *u2s, down, ssa, ssb)


def up_body(sources, rank, width, nmsg, *refs):
    first_ref = refs[0]
    msgs = refs[1 : 1 + nmsg]
    u1s = refs[1 + nmsg : 1 + nmsg + sources]
    up_ref, here_ref, side_ref, far_ref, scale_ref, lhs_ref = refs[1 + nmsg + sources :]
    tr = here_ref.shape[0]
    wide = up_ref.shape[0]
    g = pl.program_id(0)

    @pl.when(g == 0)
    def _():
        total = msgs[0][...].astype(F32)
        for m in msgs[1:]:
            total = total + m[...].astype(F32)
        lane = lax.broadcasted_iota(jnp.int32, (tr, LANES), 1)
        cell = (lax.broadcasted_iota(jnp.int32, (tr, wide), 1) // rank + first_ref[0]).astype(F32)
        for k in range(sources):
            at = k // 2 * tr
            v = total[at : at + tr]
            turned = pltpu.roll(v, rank, 1)
            v = jnp.where((lane < rank) == (k % 2 == 0), v, turned)
            v = jnp.concatenate([v] * (wide // LANES), axis=1)
            slot = jnp.concatenate([slot_column(u1s[k], tr)] * (wide // LANES), axis=1)
            lhs_ref[k] = jnp.where(cell == slot, v, 0.0).astype(BF)
        tail = total[sources // 2 * tr :]
        lane = lax.broadcasted_iota(jnp.int32, (EXT, LANES), 1)
        for b in range(tr // EXT):
            pick = (lane == 2 * b) | (lane == 2 * b + 1)
            ss = jnp.sum(jnp.where(pick, tail, 0.0), axis=1, keepdims=True)
            scale = lax.rsqrt(ss / width + EPSILON)
            scale_ref[b * EXT : (b + 1) * EXT, :] = jnp.broadcast_to(scale, (EXT, LANES))

    here_ref[...] = dot(lhs_ref[0], up_ref[...]).astype(BF)
    side_ref[:tr] = dot(lhs_ref[1], up_ref[...]).astype(BF)
    side_ref[tr:] = dot(lhs_ref[3], up_ref[...]).astype(BF)
    far_ref[...] = dot(lhs_ref[2], up_ref[...]).astype(BF)


def up_call(first, msgs, u1s, up, rank, width, tr, tile=256):
    sources = len(u1s)
    wide, features = up.shape
    whole = lambda a: pl.BlockSpec(a.shape, lambda g: (0, 0))
    cut = lambda r: pl.BlockSpec((r, tile), lambda g: (0, g))
    return pl.pallas_call(
        functools.partial(up_body, sources, rank, width, len(msgs)),
        grid=(features // tile,),
        in_specs=[pl.BlockSpec(memory_space=pltpu.SMEM)]
        + [whole(a) for a in msgs]
        + [whole(a) for a in u1s]
        + [pl.BlockSpec((wide, tile), lambda g: (0, g))],
        out_specs=[cut(tr), cut(2 * tr), cut(tr), pl.BlockSpec((tr, LANES), lambda g: (0, 0))],
        out_shape=[
            jax.ShapeDtypeStruct((tr, features), BF),
            jax.ShapeDtypeStruct((2 * tr, features), BF),
            jax.ShapeDtypeStruct((tr, features), BF),
            jax.ShapeDtypeStruct((tr, LANES), F32),
        ],
        scratch_shapes=[pltpu.VMEM((sources, tr, wide), BF)],
        compiler_params=pltpu.CompilerParams(
            dimension_semantics=("arbitrary",), vmem_limit_bytes=24 * 1024 * 1024
        ),
        cost_estimate=pl.CostEstimate(
            flops=2 * sources * tr * wide * features, bytes_accessed=2 * wide * features, transcendentals=0
        ),
        name="adapter_up",
    )(first, *msgs, *u1s, up)


def swap(a, axis, size, bit):
    return lax.ppermute(a, axis, [(i, i ^ bit) for i in range(size)])


def per_device_pairs(
    dp,
    tensor,
    row_adapter_index,
    adapter_storage_row,
    initial_head_state,
    step_head_input,
    step_gate_input,
    step_size_logits,
    state_write_key,
    state_read_query,
    head_decay_rate,
    head_skip_gain,
    gated_norm_gain,
    output_weight,
    adapter_down_weight,
    adapter_up_weight,
):
    steps, rows, width = step_head_input.shape
    tr = steps * rows
    stored, _, rank = adapter_down_weight.shape
    features = adapter_up_weight.shape[2]
    down = jnp.swapaxes(adapter_down_weight, 1, 2).reshape(stored * rank, width)
    up = adapter_up_weight.reshape(stored * rank, features)
    me = lax.axis_index("tensor")
    first = (lax.axis_index("dp") * stored)[None].astype(jnp.int32)

    state_args = (
        row_adapter_index,
        adapter_storage_row,
        initial_head_state,
        step_head_input,
        step_gate_input,
        step_size_logits,
        state_write_key,
        state_read_query,
        head_decay_rate,
        head_skip_gain,
        gated_norm_gain,
    )
    hb = 4
    carried, u1, ssa = state_call(state_args, 0, 2, hb)
    x1 = swap(u1, "dp", dp, 2)
    carried, u2, ssb = state_call(state_args, 1, 2, hb, carried)
    x2 = swap(u2, "dp", dp, 2)
    c1 = swap(u1, "dp", dp, 1)
    c2 = swap(u2, "dp", dp, 1)

    order = (me ^ jnp.array([3, 2, 1, 0], jnp.int32)).astype(jnp.int32)
    (far,) = base_call(u1, u2, output_weight, order[:1], features, [BF], 512, "base_first")
    near_in = swap(far, "tensor", tensor, 1)
    mid, near, own = base_call(u1, u2, output_weight, order[1:], features, [F32, BF, F32], 512, "base_rest")
    near_own = swap(near, "tensor", tensor, 1)
    mid_in = swap((mid + near_in.astype(F32)).astype(BF), "tensor", tensor, 2)

    d1 = swap(x1, "dp", dp, 1)
    d2 = swap(x2, "dp", dp, 1)
    u1s = [u1, c1, x1, d1]
    u2s = [u2, c2, x2, d2]
    msg = down_call(first, u1s, u2s, down, rank, ssa, ssb)
    msgs = [msg] + [swap(msg, "tensor", tensor, k) for k in range(1, tensor)]
    here, side, over, scale = up_call(first, msgs, u1s, up, rank, width * tensor, tr)
    side_in = swap(side, "dp", dp, 1)
    over_in = swap(over + side_in[tr:], "dp", dp, 2)
    total = own + near_own.astype(F32) + mid_in.astype(F32)
    total = total + here.astype(F32) + side_in[:tr].astype(F32) + over_in.astype(F32)
    mixed_out = (total * scale[:, :1]).astype(BF).reshape(steps, rows, features)
    return mixed_out, carried


def slot_lookup(row_adapter_index, adapter_storage_row):
    match = row_adapter_index[:, None] == lax.broadcasted_iota(
        jnp.int32, (row_adapter_index.shape[0], adapter_storage_row.shape[0]), 1
    )
    return jnp.sum(jnp.where(match, adapter_storage_row[None, :], 0), axis=1)


def per_device_any(
    row_adapter_index,
    adapter_storage_row,
    initial_head_state,
    step_head_input,
    step_gate_input,
    step_size_logits,
    state_write_key,
    state_read_query,
    head_decay_rate,
    head_skip_gain,
    gated_norm_gain,
    output_weight,
    adapter_down_weight,
    adapter_up_weight,
):
    steps_n, row_count, width = step_head_input.shape
    head_count = head_decay_rate.shape[0]
    head_dim = width // head_count
    carried = initial_head_state
    gated_list = []
    for moment in range(steps_n):
        delta_t = jax.nn.softplus(step_size_logits[moment])
        damping = jnp.exp(-delta_t * head_decay_rate[None, :])
        values = (
            step_head_input[moment].astype(jnp.float32).reshape(row_count, head_count, head_dim)
        )
        writer = state_write_key[moment].astype(jnp.float32)
        reader = state_read_query[moment].astype(jnp.float32)
        updated = (
            damping[:, :, None, None] * carried.astype(jnp.float32)
            + (delta_t[:, :, None] * values)[:, :, :, None] * writer[:, None, None, :]
        )
        carried = updated.astype(jnp.bfloat16)
        output = (
            jnp.sum(updated * reader[:, None, None, :], axis=3)
            + head_skip_gain[None, :, None] * values
        )
        gated_list.append(
            output.reshape(row_count, width)
            * jax.nn.silu(step_gate_input[moment].astype(jnp.float32))
        )
    gated_all = jnp.stack(gated_list)
    totals = lax.psum(jnp.sum(gated_all * gated_all, axis=2), "tensor")
    scaling = lax.rsqrt(totals / (STATE_HEADS * HEAD_WIDTH) + EPSILON)
    normed = (gated_all * scaling[:, :, None] * gated_norm_gain[None, None, :]).astype(jnp.bfloat16)
    base = jnp.dot(
        normed.reshape(steps_n * row_count, width),
        output_weight,
        preferred_element_type=jnp.float32,
    )
    base = lax.psum_scatter(
        base.reshape(steps_n, row_count, -1), "tensor", scatter_dimension=2, tiled=True
    )
    running_state = adapter_down_weight.shape[0]
    slots = slot_lookup(row_adapter_index, adapter_storage_row)
    columns = lax.broadcasted_iota(jnp.int32, (row_count, adapter_storage_row.shape[0]), 1)
    marks = (slots[:, None] == columns).astype(jnp.bfloat16)
    normed_steps_list, every_mark = (
        lax.all_gather(normed, "dp", axis=1, tiled=True),
        lax.all_gather(marks, "dp", axis=0, tiled=True),
    )
    owned = lax.dynamic_slice_in_dim(
        every_mark, lax.axis_index("dp") * running_state, running_state, 1
    )
    partial_down = jnp.einsum(
        "pcu,oue->pcoe", normed_steps_list, adapter_down_weight, preferred_element_type=jnp.float32
    )
    picked = jnp.sum(partial_down * owned.astype(jnp.float32)[None, :, :, None], axis=2)
    down_projected = lax.psum(picked, "tensor").astype(jnp.bfloat16)
    up_projected = down_projected[:, :, None, :] * owned[None, :, :, None]
    adapter_delta = jnp.einsum(
        "bcuo,uoz->bcz", up_projected, adapter_up_weight, preferred_element_type=jnp.float32
    )
    adapter_delta = lax.psum_scatter(adapter_delta, "dp", scatter_dimension=1, tiled=True)
    mixed_out = (base + adapter_delta).astype(jnp.bfloat16)
    return (mixed_out, carried)


def solution(mesh):
    placed = (
        P(("groups", "dp")),
        P(),
        P(("groups", "dp"), "tensor", None, None),
        P(None, ("groups", "dp"), "tensor"),
        P(None, ("groups", "dp"), "tensor"),
        P(None, ("groups", "dp"), "tensor"),
        P(None, ("groups", "dp"), None),
        P(None, ("groups", "dp"), None),
        P("tensor"),
        P("tensor"),
        P("tensor"),
        P("tensor", None),
        P("dp", "tensor", None),
        P("dp", None, "tensor"),
    )
    dp, tensor = mesh.shape["dp"], mesh.shape["tensor"]
    body = per_device_any
    if dp == 4 and tensor == 4:
        body = functools.partial(per_device_pairs, dp, tensor)
    return jax.shard_map(
        body,
        mesh=mesh,
        in_specs=placed,
        out_specs=(P(None, ("groups", "dp"), "tensor"), P(("groups", "dp"), "tensor", None, None)),
        check_vma=False,
    )
```

```python
import functools

import jax
import jax.numpy as jnp
from jax import lax
from jax.experimental import pallas as pl
from jax.experimental.pallas import tpu as pltpu
from jax.sharding import PartitionSpec as P

STATE_HEADS = 128
HEAD_WIDTH = 64
EPSILON = 1e-05

BF = jnp.bfloat16
F32 = jnp.float32
NT = (((1,), (1,)), ((), ()))
NN = (((1,), (0,)), ((), ()))
LANES = 128
EXT = 16
MIB = 1024 * 1024

VM = pl.BlockSpec(memory_space=pltpu.VMEM)
ANY = pl.BlockSpec(memory_space=pl.ANY)


def dot(a, b, dims=NN):
    return lax.dot_general(a, b, dims, preferred_element_type=F32)


def hbm(a):
    return pltpu.with_memory_space_constraint(a, pltpu.HBM)


def params(mib):
    return pltpu.CompilerParams(vmem_limit_bytes=mib * MIB)


def state_body(hb, *refs):
    small_src = refs[:8]
    s_ref, idx_ref, store_ref = refs[8:11]
    ns_ref, u_ref, ss_ref = refs[11:14]
    x_ref, g_ref, lg_ref, rate_ref, skip_ref, gain_ref, w_ref, q_ref = refs[14:22]
    s_buf, o_buf, chi_ref, clo_ref, wbd_ref, qbd_ref, k4_ref, xet_ref, z_ref, sq_ref = refs[22:32]
    small_sem, in_sem, out_sem, idx_buf, store_buf = refs[32:]
    steps, rows, width = x_ref.shape
    heads = lg_ref.shape[2]
    n = w_ref.shape[2]
    tr = steps * rows
    cols = hb * HEAD_WIDTH
    pairs = rows // 2
    chunks = heads // hb

    def state_in(c):
        return pltpu.make_async_copy(
            s_ref.at[:, pl.ds(c * hb, hb)], s_buf.at[:, pl.ds(c * hb, hb)], in_sem.at[c]
        )

    def state_out(c):
        return pltpu.make_async_copy(
            o_buf.at[:, pl.ds(c * hb, hb)], ns_ref.at[:, pl.ds(c * hb, hb)], out_sem.at[c]
        )

    small_dst = [x_ref, g_ref, lg_ref, rate_ref, skip_ref, gain_ref, w_ref, q_ref, idx_buf, store_buf]
    small_src = list(small_src) + [idx_ref, store_ref]
    copies = [
        pltpu.make_async_copy(a, b, small_sem.at[i]) for i, (a, b) in enumerate(zip(small_src, small_dst))
    ]
    for i in (2, 3, 4, 6, 7, 0):
        copies[i].start()
    state_in(0).start()
    for i in (1, 5, 8, 9):
        copies[i].start()
    for c in range(1, chunks):
        state_in(c).start()
    for i in (2, 3, 4, 6, 7):
        copies[i].wait()

    delta = [jax.nn.softplus(lg_ref[t]) for t in range(steps)]
    keep = [jnp.exp(-delta[t] * rate_ref[...]) for t in range(steps)]
    w = [w_ref[t].astype(F32) for t in range(steps)]
    q = [q_ref[t].astype(F32) for t in range(steps)]
    cum = []
    for t in range(steps):
        cum.append(keep[t] if t == 0 else cum[-1] * keep[t])
    coef = list(cum)
    cur = []
    for t in range(steps):
        cur = [v * keep[t] for v in cur] + [delta[t]]
        for s in range(t + 1):
            a = cur[s] * jnp.sum(w[s] * q[t], axis=1, keepdims=True)
            if s == t:
                a = a + skip_ref[...]
            coef.append(a)
    coef = jnp.concatenate(cur + coef, axis=0)
    hi = coef.astype(BF)
    chi_ref[...] = hi
    clo_ref[...] = (coef - hi.astype(F32)).astype(BF)
    eye = lax.broadcasted_iota(jnp.int32, (heads, heads), 0) == lax.broadcasted_iota(
        jnp.int32, (heads, heads), 1
    )
    for r in range(rows):
        col = jnp.sum(jnp.where(eye, cum[-1][r : r + 1, :], 0.0), axis=1, keepdims=True)
        k4_ref[r] = jnp.broadcast_to(col, (heads, LANES))
    wf = jnp.concatenate(w, axis=0)
    qf = jnp.concatenate(q, axis=0)
    owner = lax.rem(lax.broadcasted_iota(jnp.int32, (tr, n), 0), rows)
    for p in range(pairs):
        for half in range(2):
            mine = owner == 2 * p + half
            wbd_ref[p, :, half * n : (half + 1) * n] = jnp.where(mine, wf, 0.0).astype(BF)
            qbd_ref[p, :, half * n : (half + 1) * n] = jnp.where(mine, qf, 0.0).astype(BF)

    hsel = lax.broadcasted_iota(jnp.int32, (heads, cols), 0)
    hcol = lax.broadcasted_iota(jnp.int32, (heads, cols), 1) // HEAD_WIDTH

    def spread(c, at):
        expand = jnp.where(hsel == hcol + c * hb, 1.0, 0.0).astype(BF)
        return dot(chi_ref[at], expand) + dot(clo_ref[at], expand)

    def columns(c):
        return pl.ds(pl.multiple_of(c * cols, cols), cols)

    def inputs(c):
        return [x_ref[t, :, columns(c)].astype(F32) for t in range(steps)]

    def scaled_inputs(c):
        e = spread(c, slice(0, tr))
        x = inputs(c)
        xe = jnp.concatenate([e[s * rows : (s + 1) * rows] * x[s] for s in range(steps)], axis=0)
        xet_ref[lax.rem(c, 2)] = xe.T.astype(BF)

    def gated_rows(c):
        z = z_ref[lax.rem(c, 2)]
        ce = spread(c, slice(tr, None))
        x = inputs(c)
        gain = gain_ref[:, columns(c)]
        at = tr
        out_rows = []
        for t in range(steps):
            y = ce[t * rows : (t + 1) * rows] * z[t * rows : (t + 1) * rows]
            for s in range(t + 1):
                y = y + ce[at : at + rows] * x[s]
                at += rows
            g = g_ref[t, :, columns(c)].astype(F32)
            gated = y * (g / (1.0 + jnp.exp(-g)))
            sq = gated * gated
            part = sq[:, :LANES]
            for b in range(1, cols // LANES):
                part = part + sq[:, b * LANES : (b + 1) * LANES]
            sq_ref[c, t * rows : (t + 1) * rows, :] = part
            out_rows.append(gated * gain)
        u_ref[:, columns(c)] = jnp.concatenate(out_rows, axis=0).astype(BF)

    for i in (0, 1, 5, 8, 9):
        copies[i].wait()
    scaled_inputs(0)
    z_ref[...] = jnp.zeros_like(z_ref)

    def chunk(c, carry):
        state_in(c).wait()
        xet = xet_ref[lax.rem(c, 2)]
        z = jnp.zeros((tr, cols), F32)
        for p in range(pairs):
            s0 = s_buf[2 * p, pl.ds(c * hb, hb)].reshape(cols, n)
            s1 = s_buf[2 * p + 1, pl.ds(c * hb, hb)].reshape(cols, n)
            z = z + dot(qbd_ref[p], jnp.concatenate([s0, s1], axis=1), NT)
            up = dot(xet, wbd_ref[p])
            for half, sv in ((0, s0), (1, s1)):
                r = 2 * p + half
                k4 = k4_ref[r, pl.ds(c * hb, hb), :]
                grown = (
                    k4[:, None, :] * sv.astype(F32).reshape(hb, HEAD_WIDTH, n)
                    + up[:, half * n : (half + 1) * n].reshape(hb, HEAD_WIDTH, n)
                )
                o_buf[r, pl.ds(c * hb, hb)] = grown.astype(BF)
        scaled_inputs(jnp.minimum(c + 1, chunks - 1))
        gated_rows(jnp.maximum(c - 1, 0))
        z_ref[lax.rem(c, 2)] = z
        state_out(c).start()
        return carry

    lax.fori_loop(0, chunks, chunk, 0)
    gated_rows(chunks - 1)
    total = sq_ref[0]
    for c in range(1, chunks):
        total = total + sq_ref[c]
    ss_ref[...] = total
    which = lax.rem(lax.broadcasted_iota(jnp.int32, (tr, LANES), 0), rows)
    slots = jnp.zeros((tr, LANES), F32)
    for r in range(rows):
        slots = jnp.where(which == r, store_buf[idx_buf[r]].astype(F32), slots)
    u_ref[:, width:] = slots.astype(BF)
    for c in range(chunks):
        state_out(c).wait()


def state_call(args, hb):
    (idx, store, state, x, g, lg, w, q, rate, skip, gain) = args
    steps, rows, width = x.shape
    heads = rate.shape[1]
    tr = steps * rows
    n = w.shape[2]
    cols = hb * HEAD_WIDTH
    chunks = heads // hb
    operands = [x, g, lg, rate, skip, gain, w, q, state, idx, store]
    coef_rows = (steps * (steps + 1) // 2 + 2 * steps) * rows
    scratch = [
        pltpu.VMEM(x.shape, BF),
        pltpu.VMEM(g.shape, BF),
        pltpu.VMEM(lg.shape, F32),
        pltpu.VMEM(rate.shape, F32),
        pltpu.VMEM(skip.shape, F32),
        pltpu.VMEM(gain.shape, F32),
        pltpu.VMEM(w.shape, BF),
        pltpu.VMEM(q.shape, BF),
        pltpu.VMEM(state.shape, BF),
        pltpu.VMEM(state.shape, BF),
        pltpu.VMEM((coef_rows, heads), BF),
        pltpu.VMEM((coef_rows, heads), BF),
        pltpu.VMEM((rows // 2, tr, 2 * n), BF),
        pltpu.VMEM((rows // 2, tr, 2 * n), BF),
        pltpu.VMEM((rows, heads, LANES), F32),
        pltpu.VMEM((2, cols, tr), BF),
        pltpu.VMEM((2, tr, cols), F32),
        pltpu.VMEM((chunks, tr, LANES), F32),
        pltpu.SemaphoreType.DMA((10,)),
        pltpu.SemaphoreType.DMA((chunks,)),
        pltpu.SemaphoreType.DMA((chunks,)),
        pltpu.SMEM(idx.shape, jnp.int32),
        pltpu.SMEM(store.shape, jnp.int32),
    ]
    return pl.pallas_call(
        functools.partial(state_body, hb),
        in_specs=[ANY] * len(operands),
        out_specs=[ANY, VM, VM],
        out_shape=[
            jax.ShapeDtypeStruct(state.shape, BF),
            jax.ShapeDtypeStruct((tr, width + LANES), BF),
            jax.ShapeDtypeStruct((tr, LANES), F32),
        ],
        scratch_shapes=scratch,
        compiler_params=params(36),
        cost_estimate=pl.CostEstimate(
            flops=4 * tr * rows * heads * HEAD_WIDTH * n, bytes_accessed=4 * state.size, transcendentals=0
        ),
        name="state_steps",
    )(*operands)


def base_body(flips, features, u_ref, w_ref, *refs):
    outs = refs[: len(flips)]
    buf, acc, sems = refs[len(flips) :]
    pieces = buf.shape[1]
    depth = buf.shape[2]
    me = lax.axis_index("tensor")

    def fetch(k, i):
        at = pl.multiple_of((me ^ flips[k]) * features, LANES)
        return pltpu.make_async_copy(
            w_ref.at[pl.ds(i * depth, depth), pl.ds(at, features)], buf.at[k, i], sems.at[k, i]
        )

    for k in range(len(flips)):
        for i in range(pieces):
            fetch(k, i).start()
    for k in range(len(flips)):
        for i in range(pieces):
            fetch(k, i).wait()
            tile = dot(u_ref[:, i * depth : (i + 1) * depth], buf[k, i])
            if i == 0:
                acc[...] = tile
            elif i < pieces - 1:
                acc[...] += tile
            else:
                outs[k][...] = (acc[...] + tile).astype(outs[k].dtype)


def base_call(u, weight, flips, types, features, name):
    tr = u.shape[0]
    depth = weight.shape[0]
    pieces = 4
    count = len(flips)
    return pl.pallas_call(
        functools.partial(base_body, flips, features),
        in_specs=[VM, ANY],
        out_specs=[VM] * count,
        out_shape=[jax.ShapeDtypeStruct((tr, features), t) for t in types],
        scratch_shapes=[
            pltpu.VMEM((count, pieces, depth // pieces, features), BF),
            pltpu.VMEM((tr, features), F32),
            pltpu.SemaphoreType.DMA((count, pieces)),
        ],
        compiler_params=params(20),
        cost_estimate=pl.CostEstimate(
            flops=2 * tr * depth * features * count,
            bytes_accessed=2 * depth * features * count,
            transcendentals=0,
        ),
        name=name,
    )(u, weight)


def down_body(sources, rank, *refs):
    us = refs[:sources]
    down_ref, ss_ref, out_ref, rows_ref = refs[sources:]
    tr = us[0].shape[0]
    wide, width = down_ref.shape
    first = lax.axis_index("dp") * (wide // rank)
    pad = jnp.zeros((LANES - tr, LANES), F32)
    slots = []
    for k in range(sources):
        rows_ref[k, :tr] = us[k][:, :width]
        rows_ref[k, tr:] = jnp.zeros((LANES - tr, width), BF)
        column = jnp.concatenate([us[k][:, width:].astype(F32), pad - 1.0], axis=0)
        slots.append(column.T[:1])
    slots = jnp.concatenate(slots, axis=1)
    lanes = sources * LANES
    cell = lax.broadcasted_iota(jnp.int32, (wide, lanes), 0) // rank + first
    part = dot(down_ref[...], rows_ref[...].reshape(lanes, width), NT)
    part = jnp.where(cell.astype(F32) == slots, part, 0.0)
    total = part[:rank]
    for a in range(1, wide // rank):
        total = total + part[a * rank : (a + 1) * rank]
    ss = jnp.sum(jnp.concatenate([ss_ref[...], pad], axis=0).T, axis=0, keepdims=True)
    hi = ss.astype(BF).astype(F32)
    gap = jnp.zeros((1, lanes - LANES), F32)
    row = lax.broadcasted_iota(jnp.int32, (EXT, lanes), 0)
    tail = jnp.where(row == 0, slots, 0.0)
    tail = jnp.where(row == 1, jnp.concatenate([hi, gap], axis=1), tail)
    tail = jnp.where(row == 2, jnp.concatenate([ss - hi, gap], axis=1), tail)
    out_ref[:rank] = total.astype(BF)
    out_ref[rank:] = tail.astype(BF)


def down_call(us, down, rank, ss):
    sources = len(us)
    tr = us[0].shape[0]
    wide, width = down.shape
    return pl.pallas_call(
        functools.partial(down_body, sources, rank),
        in_specs=[VM] * (sources + 2),
        out_specs=VM,
        out_shape=jax.ShapeDtypeStruct((rank + EXT, sources * LANES), BF),
        scratch_shapes=[pltpu.VMEM((sources, LANES, width), BF)],
        compiler_params=params(20),
        cost_estimate=pl.CostEstimate(
            flops=2 * sources * tr * wide * width, bytes_accessed=2 * wide * width, transcendentals=0
        ),
        name="adapter_down",
    )(*us, down, ss)


def up_body(rank, width, nmsg, *refs):
    msgs = refs[:nmsg]
    up_ref, here_ref, side_ref, far_ref, scale_ref, lhs_ref = refs[nmsg:]
    tr = here_ref.shape[0]
    wide = up_ref.shape[0]
    sources = lhs_ref.shape[0]
    total = msgs[0][:rank].astype(F32)
    tail = msgs[0][rank:].astype(F32)
    slots = tail[:1]
    for m in msgs[1:]:
        total = total + m[:rank].astype(F32)
        tail = tail + m[rank:].astype(F32)
    squares = tail[1:2, :LANES] + tail[2:3, :LANES]
    scale = lax.rsqrt(squares / width + EPSILON)
    scale = jnp.concatenate([scale, jnp.zeros((7, LANES), F32)], axis=0).T
    scale_ref[...] = jnp.broadcast_to(scale[:tr, :1], (tr, LANES))
    first = lax.axis_index("dp") * (wide // rank)
    cell = (lax.broadcasted_iota(jnp.int32, (tr, wide), 1) // rank + first).astype(F32)
    for k in range(sources):
        mine = slice(k * LANES, (k + 1) * LANES)
        twice = jnp.concatenate([total[:, mine], total[:, mine]], axis=0).T[:tr]
        slot = jnp.broadcast_to(slots[:, mine], (8, LANES)).T[:tr, :1]
        spread = jnp.concatenate([twice] * (wide // LANES), axis=1)
        lhs_ref[k] = jnp.where(cell == slot, spread, 0.0).astype(BF)
    delta = dot(lhs_ref[...].reshape(sources * tr, wide), up_ref[...])
    here_ref[...] = delta[:tr].astype(BF)
    side_ref[:tr] = delta[tr : 2 * tr].astype(BF)
    far_ref[...] = delta[2 * tr : 3 * tr].astype(BF)
    side_ref[tr:] = delta[3 * tr :].astype(BF)


def up_call(msgs, up, rank, width, tr):
    sources = msgs[0].shape[1] // LANES
    wide, features = up.shape
    return pl.pallas_call(
        functools.partial(up_body, rank, width, len(msgs)),
        in_specs=[VM] * (len(msgs) + 1),
        out_specs=[VM] * 4,
        out_shape=[
            jax.ShapeDtypeStruct((tr, features), BF),
            jax.ShapeDtypeStruct((2 * tr, features), BF),
            jax.ShapeDtypeStruct((tr, features), BF),
            jax.ShapeDtypeStruct((tr, LANES), F32),
        ],
        scratch_shapes=[pltpu.VMEM((sources, tr, wide), BF)],
        compiler_params=params(16),
        cost_estimate=pl.CostEstimate(
            flops=2 * sources * tr * wide * features, bytes_accessed=2 * wide * features, transcendentals=0
        ),
        name="adapter_up",
    )(*msgs, up)


def swap(a, axis, size, bit):
    return lax.ppermute(a, axis, [(i, i ^ bit) for i in range(size)])


def after(a, *others):
    return lax.optimization_barrier((a,) + others)[0]


def per_device_pairs(
    dp,
    tensor,
    row_adapter_index,
    adapter_storage_row,
    initial_head_state,
    step_head_input,
    step_gate_input,
    step_size_logits,
    state_write_key,
    state_read_query,
    head_decay_rate,
    head_skip_gain,
    gated_norm_gain,
    output_weight,
    adapter_down_weight,
    adapter_up_weight,
):
    steps, rows, width = step_head_input.shape
    tr = steps * rows
    stored, _, rank = adapter_down_weight.shape
    features = adapter_up_weight.shape[2]
    down = jnp.swapaxes(adapter_down_weight, 1, 2).reshape(stored * rank, width)
    up = adapter_up_weight.reshape(stored * rank, features)
    weight = hbm(output_weight)
    state_args = (
        hbm(row_adapter_index),
        hbm(adapter_storage_row),
        hbm(initial_head_state),
        hbm(step_head_input),
        hbm(step_gate_input),
        hbm(step_size_logits),
        hbm(state_write_key),
        hbm(state_read_query),
        hbm(head_decay_rate[None]),
        hbm(head_skip_gain[None]),
        hbm(gated_norm_gain[None]),
    )
    carried, u, ss = state_call(state_args, 8)
    far_u = swap(u, "dp", dp, 2)
    near_u = swap(u, "dp", dp, 1)
    (far,) = base_call(u, weight, (3,), [BF], features, "base_first")
    near_in = swap(far, "tensor", tensor, 1)
    mid, near, own = base_call(after(u, far), weight, (2, 1, 0), [F32, BF, F32], features, "base_rest")
    both_u = swap(after(far_u, own), "dp", dp, 1)
    near_own = swap(near, "tensor", tensor, 1)
    mid = (mid + near_in.astype(F32)).astype(BF)
    mid_in = swap(mid, "tensor", tensor, 2)
    msg = down_call([after(u, mid), near_u, far_u, both_u], down, rank, ss)
    msgs = [msg] + [swap(msg, "tensor", tensor, k) for k in range(1, tensor)]
    here, side, over, scale = up_call(msgs, up, rank, width * tensor, tr)
    side_in = swap(side, "dp", dp, 1)
    over_in = swap(over + side_in[tr:], "dp", dp, 2)
    total = own + near_own.astype(F32) + mid_in.astype(F32)
    total = total + here.astype(F32) + side_in[:tr].astype(F32) + over_in.astype(F32)
    mixed_out = (total * scale[:, :1]).astype(BF).reshape(steps, rows, features)
    return mixed_out, carried


def slot_lookup(row_adapter_index, adapter_storage_row):
    match = row_adapter_index[:, None] == lax.broadcasted_iota(
        jnp.int32, (row_adapter_index.shape[0], adapter_storage_row.shape[0]), 1
    )
    return jnp.sum(jnp.where(match, adapter_storage_row[None, :], 0), axis=1)


def per_device_any(
    row_adapter_index,
    adapter_storage_row,
    initial_head_state,
    step_head_input,
    step_gate_input,
    step_size_logits,
    state_write_key,
    state_read_query,
    head_decay_rate,
    head_skip_gain,
    gated_norm_gain,
    output_weight,
    adapter_down_weight,
    adapter_up_weight,
):
    steps_n, row_count, width = step_head_input.shape
    head_count = head_decay_rate.shape[0]
    head_dim = width // head_count
    carried = initial_head_state
    gated_list = []
    for moment in range(steps_n):
        delta_t = jax.nn.softplus(step_size_logits[moment])
        damping = jnp.exp(-delta_t * head_decay_rate[None, :])
        values = (
            step_head_input[moment].astype(jnp.float32).reshape(row_count, head_count, head_dim)
        )
        writer = state_write_key[moment].astype(jnp.float32)
        reader = state_read_query[moment].astype(jnp.float32)
        updated = (
            damping[:, :, None, None] * carried.astype(jnp.float32)
            + (delta_t[:, :, None] * values)[:, :, :, None] * writer[:, None, None, :]
        )
        carried = updated.astype(jnp.bfloat16)
        output = (
            jnp.sum(updated * reader[:, None, None, :], axis=3)
            + head_skip_gain[None, :, None] * values
        )
        gated_list.append(
            output.reshape(row_count, width)
            * jax.nn.silu(step_gate_input[moment].astype(jnp.float32))
        )
    gated_all = jnp.stack(gated_list)
    totals = lax.psum(jnp.sum(gated_all * gated_all, axis=2), "tensor")
    scaling = lax.rsqrt(totals / (STATE_HEADS * HEAD_WIDTH) + EPSILON)
    normed = (gated_all * scaling[:, :, None] * gated_norm_gain[None, None, :]).astype(jnp.bfloat16)
    base = jnp.dot(
        normed.reshape(steps_n * row_count, width),
        output_weight,
        preferred_element_type=jnp.float32,
    )
    base = lax.psum_scatter(
        base.reshape(steps_n, row_count, -1), "tensor", scatter_dimension=2, tiled=True
    )
    running_state = adapter_down_weight.shape[0]
    slots = slot_lookup(row_adapter_index, adapter_storage_row)
    columns = lax.broadcasted_iota(jnp.int32, (row_count, adapter_storage_row.shape[0]), 1)
    marks = (slots[:, None] == columns).astype(jnp.bfloat16)
    normed_steps_list, every_mark = (
        lax.all_gather(normed, "dp", axis=1, tiled=True),
        lax.all_gather(marks, "dp", axis=0, tiled=True),
    )
    owned = lax.dynamic_slice_in_dim(
        every_mark, lax.axis_index("dp") * running_state, running_state, 1
    )
    partial_down = jnp.einsum(
        "pcu,oue->pcoe", normed_steps_list, adapter_down_weight, preferred_element_type=jnp.float32
    )
    picked = jnp.sum(partial_down * owned.astype(jnp.float32)[None, :, :, None], axis=2)
    down_projected = lax.psum(picked, "tensor").astype(jnp.bfloat16)
    up_projected = down_projected[:, :, None, :] * owned[None, :, :, None]
    adapter_delta = jnp.einsum(
        "bcuo,uoz->bcz", up_projected, adapter_up_weight, preferred_element_type=jnp.float32
    )
    adapter_delta = lax.psum_scatter(adapter_delta, "dp", scatter_dimension=1, tiled=True)
    mixed_out = (base + adapter_delta).astype(jnp.bfloat16)
    return (mixed_out, carried)


def solution(mesh):
    placed = (
        P(("groups", "dp")),
        P(),
        P(("groups", "dp"), "tensor", None, None),
        P(None, ("groups", "dp"), "tensor"),
        P(None, ("groups", "dp"), "tensor"),
        P(None, ("groups", "dp"), "tensor"),
        P(None, ("groups", "dp"), None),
        P(None, ("groups", "dp"), None),
        P("tensor"),
        P("tensor"),
        P("tensor"),
        P("tensor", None),
        P("dp", "tensor", None),
        P("dp", None, "tensor"),
    )
    dp, tensor = mesh.shape["dp"], mesh.shape["tensor"]
    body = per_device_any
    if dp == 4 and tensor == 4:
        body = functools.partial(per_device_pairs, dp, tensor)
    return jax.shard_map(
        body,
        mesh=mesh,
        in_specs=placed,
        out_specs=(P(None, ("groups", "dp"), "tensor"), P(("groups", "dp"), "tensor", None, None)),
        check_vma=False,
    )
```

```python
import functools

import jax
import jax.numpy as jnp
from jax import lax
from jax.experimental import pallas as pl
from jax.experimental.pallas import tpu as pltpu
from jax.sharding import PartitionSpec as P

STATE_HEADS = 128
HEAD_WIDTH = 64
EPSILON = 1e-05

BF = jnp.bfloat16
F32 = jnp.float32
NT = (((1,), (1,)), ((), ()))
NN = (((1,), (0,)), ((), ()))
LANES = 128
EXT = 16
MIB = 1024 * 1024

VM = pl.BlockSpec(memory_space=pltpu.VMEM)
ANY = pl.BlockSpec(memory_space=pl.ANY)


def dot(a, b, dims=NN):
    return lax.dot_general(a, b, dims, preferred_element_type=F32)


def hbm(a):
    return pltpu.with_memory_space_constraint(a, pltpu.HBM)


def params(mib):
    return pltpu.CompilerParams(vmem_limit_bytes=mib * MIB)


def state_body(hb, *refs):
    small_src = refs[:8]
    s_ref, idx_ref, store_ref = refs[8:11]
    ns_ref, u_ref, ss_ref = refs[11:14]
    x_ref, g_ref, lg_ref, rate_ref, skip_ref, gain_ref, w_ref, q_ref = refs[14:22]
    s_buf, o_buf, chi_ref, clo_ref, wbd_ref, qbd_ref, k4_ref, xet_ref, z_ref, sq_ref = refs[22:32]
    small_sem, in_sem, out_sem, idx_buf, store_buf = refs[32:]
    steps, rows, width = x_ref.shape
    heads = lg_ref.shape[2]
    n = w_ref.shape[2]
    tr = steps * rows
    cols = hb * HEAD_WIDTH
    pairs = rows // 2
    chunks = heads // hb

    def state_in(c):
        return pltpu.make_async_copy(
            s_ref.at[:, pl.ds(c * hb, hb)], s_buf.at[:, pl.ds(c * hb, hb)], in_sem.at[c]
        )

    def state_out(c):
        return pltpu.make_async_copy(
            o_buf.at[:, pl.ds(c * hb, hb)], ns_ref.at[:, pl.ds(c * hb, hb)], out_sem.at[c]
        )

    small_dst = [x_ref, g_ref, lg_ref, rate_ref, skip_ref, gain_ref, w_ref, q_ref, idx_buf, store_buf]
    small_src = list(small_src) + [idx_ref, store_ref]
    copies = [
        pltpu.make_async_copy(a, b, small_sem.at[i]) for i, (a, b) in enumerate(zip(small_src, small_dst))
    ]
    for i in (2, 3, 4, 6, 7, 0):
        copies[i].start()
    state_in(0).start()
    for i in (1, 5, 8, 9):
        copies[i].start()
    for c in range(1, chunks):
        state_in(c).start()
    for i in (2, 3, 4, 6, 7):
        copies[i].wait()

    delta = [jax.nn.softplus(lg_ref[t]) for t in range(steps)]
    keep = [jnp.exp(-delta[t] * rate_ref[...]) for t in range(steps)]
    w = [w_ref[t].astype(F32) for t in range(steps)]
    q = [q_ref[t].astype(F32) for t in range(steps)]
    cum = []
    for t in range(steps):
        cum.append(keep[t] if t == 0 else cum[-1] * keep[t])
    coef = list(cum)
    cur = []
    for t in range(steps):
        cur = [v * keep[t] for v in cur] + [delta[t]]
        for s in range(t + 1):
            a = cur[s] * jnp.sum(w[s] * q[t], axis=1, keepdims=True)
            if s == t:
                a = a + skip_ref[...]
            coef.append(a)
    coef = jnp.concatenate(cur + coef, axis=0)
    hi = coef.astype(BF)
    chi_ref[...] = hi
    clo_ref[...] = (coef - hi.astype(F32)).astype(BF)
    eye = lax.broadcasted_iota(jnp.int32, (heads, heads), 0) == lax.broadcasted_iota(
        jnp.int32, (heads, heads), 1
    )
    for r in range(rows):
        col = jnp.sum(jnp.where(eye, cum[-1][r : r + 1, :], 0.0), axis=1, keepdims=True)
        k4_ref[r] = jnp.broadcast_to(col, (heads, LANES))
    wf = jnp.concatenate(w, axis=0)
    qf = jnp.concatenate(q, axis=0)
    owner = lax.rem(lax.broadcasted_iota(jnp.int32, (tr, n), 0), rows)
    for p in range(pairs):
        for half in range(2):
            mine = owner == 2 * p + half
            wbd_ref[p, :, half * n : (half + 1) * n] = jnp.where(mine, wf, 0.0).astype(BF)
            qbd_ref[p, :, half * n : (half + 1) * n] = jnp.where(mine, qf, 0.0).astype(BF)

    hsel = lax.broadcasted_iota(jnp.int32, (heads, cols), 0)
    hcol = lax.broadcasted_iota(jnp.int32, (heads, cols), 1) // HEAD_WIDTH

    def spread(c, at):
        expand = jnp.where(hsel == hcol + c * hb, 1.0, 0.0).astype(BF)
        return dot(chi_ref[at], expand) + dot(clo_ref[at], expand)

    def columns(c):
        return pl.ds(pl.multiple_of(c * cols, cols), cols)

    def inputs(c):
        return [x_ref[t, :, columns(c)].astype(F32) for t in range(steps)]

    def scaled_inputs(c):
        e = spread(c, slice(0, tr))
        x = inputs(c)
        xe = jnp.concatenate([e[s * rows : (s + 1) * rows] * x[s] for s in range(steps)], axis=0)
        xet_ref[lax.rem(c, 2)] = xe.T.astype(BF)

    def gated_rows(c):
        z = z_ref[lax.rem(c, 2)]
        ce = spread(c, slice(tr, None))
        x = inputs(c)
        gain = gain_ref[:, columns(c)]
        at = tr
        out_rows = []
        for t in range(steps):
            y = ce[t * rows : (t + 1) * rows] * z[t * rows : (t + 1) * rows]
            for s in range(t + 1):
                y = y + ce[at : at + rows] * x[s]
                at += rows
            g = g_ref[t, :, columns(c)].astype(F32)
            gated = y * (g / (1.0 + jnp.exp(-g)))
            sq = gated * gated
            part = sq[:, :LANES]
            for b in range(1, cols // LANES):
                part = part + sq[:, b * LANES : (b + 1) * LANES]
            sq_ref[c, t * rows : (t + 1) * rows, :] = part
            out_rows.append(gated * gain)
        u_ref[:, columns(c)] = jnp.concatenate(out_rows, axis=0).astype(BF)

    for i in (0, 1, 5, 8, 9):
        copies[i].wait()
    scaled_inputs(0)
    z_ref[...] = jnp.zeros_like(z_ref)

    def chunk(c, carry):
        state_in(c).wait()
        xet = xet_ref[lax.rem(c, 2)]
        z = jnp.zeros((tr, cols), F32)
        for p in range(pairs):
            s0 = s_buf[2 * p, pl.ds(c * hb, hb)].reshape(cols, n)
            s1 = s_buf[2 * p + 1, pl.ds(c * hb, hb)].reshape(cols, n)
            z = z + dot(qbd_ref[p], jnp.concatenate([s0, s1], axis=1), NT)
            up = dot(xet, wbd_ref[p])
            for half, sv in ((0, s0), (1, s1)):
                r = 2 * p + half
                k4 = k4_ref[r, pl.ds(c * hb, hb), :]
                grown = (
                    k4[:, None, :] * sv.astype(F32).reshape(hb, HEAD_WIDTH, n)
                    + up[:, half * n : (half + 1) * n].reshape(hb, HEAD_WIDTH, n)
                )
                o_buf[r, pl.ds(c * hb, hb)] = grown.astype(BF)
        scaled_inputs(jnp.minimum(c + 1, chunks - 1))
        gated_rows(jnp.maximum(c - 1, 0))
        z_ref[lax.rem(c, 2)] = z
        state_out(c).start()
        return carry

    lax.fori_loop(0, chunks, chunk, 0)
    gated_rows(chunks - 1)
    total = sq_ref[0]
    for c in range(1, chunks):
        total = total + sq_ref[c]
    ss_ref[...] = total
    which = lax.rem(lax.broadcasted_iota(jnp.int32, (tr, LANES), 0), rows)
    slots = jnp.zeros((tr, LANES), F32)
    for r in range(rows):
        slots = jnp.where(which == r, store_buf[idx_buf[r]].astype(F32), slots)
    u_ref[:, width:] = slots.astype(BF)
    for c in range(chunks):
        state_out(c).wait()


def state_call(args, hb):
    (idx, store, state, x, g, lg, w, q, rate, skip, gain) = args
    steps, rows, width = x.shape
    heads = rate.shape[1]
    tr = steps * rows
    n = w.shape[2]
    cols = hb * HEAD_WIDTH
    chunks = heads // hb
    operands = [x, g, lg, rate, skip, gain, w, q, state, idx, store]
    coef_rows = (steps * (steps + 1) // 2 + 2 * steps) * rows
    scratch = [
        pltpu.VMEM(x.shape, BF),
        pltpu.VMEM(g.shape, BF),
        pltpu.VMEM(lg.shape, F32),
        pltpu.VMEM(rate.shape, F32),
        pltpu.VMEM(skip.shape, F32),
        pltpu.VMEM(gain.shape, F32),
        pltpu.VMEM(w.shape, BF),
        pltpu.VMEM(q.shape, BF),
        pltpu.VMEM(state.shape, BF),
        pltpu.VMEM(state.shape, BF),
        pltpu.VMEM((coef_rows, heads), BF),
        pltpu.VMEM((coef_rows, heads), BF),
        pltpu.VMEM((rows // 2, tr, 2 * n), BF),
        pltpu.VMEM((rows // 2, tr, 2 * n), BF),
        pltpu.VMEM((rows, heads, LANES), F32),
        pltpu.VMEM((2, cols, tr), BF),
        pltpu.VMEM((2, tr, cols), F32),
        pltpu.VMEM((chunks, tr, LANES), F32),
        pltpu.SemaphoreType.DMA((10,)),
        pltpu.SemaphoreType.DMA((chunks,)),
        pltpu.SemaphoreType.DMA((chunks,)),
        pltpu.SMEM(idx.shape, jnp.int32),
        pltpu.SMEM(store.shape, jnp.int32),
    ]
    return pl.pallas_call(
        functools.partial(state_body, hb),
        in_specs=[ANY] * len(operands),
        out_specs=[ANY, VM, VM],
        out_shape=[
            jax.ShapeDtypeStruct(state.shape, BF),
            jax.ShapeDtypeStruct((tr, width + LANES), BF),
            jax.ShapeDtypeStruct((tr, LANES), F32),
        ],
        scratch_shapes=scratch,
        compiler_params=params(36),
        cost_estimate=pl.CostEstimate(
            flops=4 * tr * rows * heads * HEAD_WIDTH * n, bytes_accessed=4 * state.size, transcendentals=0
        ),
        name="state_steps",
    )(*operands)


def base_body(flips, features, u_ref, w_ref, *refs):
    outs = refs[: len(flips)]
    buf, acc, sems = refs[len(flips) :]
    pieces = buf.shape[1]
    depth = buf.shape[2]
    me = lax.axis_index("tensor")

    def fetch(k, i):
        at = pl.multiple_of((me ^ flips[k]) * features, LANES)
        return pltpu.make_async_copy(
            w_ref.at[pl.ds(i * depth, depth), pl.ds(at, features)], buf.at[k, i], sems.at[k, i]
        )

    for k in range(len(flips)):
        for i in range(pieces):
            fetch(k, i).start()
    for k in range(len(flips)):
        for i in range(pieces):
            fetch(k, i).wait()
            tile = dot(u_ref[:, i * depth : (i + 1) * depth], buf[k, i])
            if i == 0:
                acc[...] = tile
            elif i < pieces - 1:
                acc[...] += tile
            else:
                outs[k][...] = (acc[...] + tile).astype(outs[k].dtype)


def base_call(u, weight, flips, types, features, name):
    tr = u.shape[0]
    depth = weight.shape[0]
    pieces = 4
    count = len(flips)
    return pl.pallas_call(
        functools.partial(base_body, flips, features),
        in_specs=[VM, ANY],
        out_specs=[VM] * count,
        out_shape=[jax.ShapeDtypeStruct((tr, features), t) for t in types],
        scratch_shapes=[
            pltpu.VMEM((count, pieces, depth // pieces, features), BF),
            pltpu.VMEM((tr, features), F32),
            pltpu.SemaphoreType.DMA((count, pieces)),
        ],
        compiler_params=params(20),
        cost_estimate=pl.CostEstimate(
            flops=2 * tr * depth * features * count,
            bytes_accessed=2 * depth * features * count,
            transcendentals=0,
        ),
        name=name,
    )(u, weight)


def down_body(sources, rank, *refs):
    us = refs[:sources]
    down_ref, ss_ref, out_ref, rows_ref = refs[sources:]
    tr = us[0].shape[0]
    wide, width = down_ref.shape
    lanes = sources * tr
    first = lax.axis_index("dp") * (wide // rank)
    slots = []
    for k in range(sources):
        rows_ref[k * tr : (k + 1) * tr] = us[k][:, :width]
        slots.append(us[k][:, width:].astype(F32))
    slots = jnp.concatenate(slots, axis=0).T[:1]
    cell = lax.broadcasted_iota(jnp.int32, (wide, lanes), 0) // rank + first
    part = dot(down_ref[...], rows_ref[...], NT)
    part = jnp.where(cell.astype(F32) == slots, part, 0.0)
    total = part[:rank]
    for a in range(1, wide // rank):
        total = total + part[a * rank : (a + 1) * rank]
    ss = jnp.sum(ss_ref[...].T, axis=0, keepdims=True)
    hi = ss.astype(BF).astype(F32)
    gap = jnp.zeros((1, lanes - tr), F32)
    row = lax.broadcasted_iota(jnp.int32, (EXT, lanes), 0)
    at = 1 + 2 * lax.rem(lax.axis_index("tensor"), 2)
    tail = jnp.where(row == 0, slots, 0.0)
    tail = jnp.where(row == at, jnp.concatenate([hi, gap], axis=1), tail)
    tail = jnp.where(row == at + 1, jnp.concatenate([ss - hi, gap], axis=1), tail)
    out_ref[:rank] = total.astype(BF)
    out_ref[rank:] = tail.astype(BF)


def down_call(us, down, rank, ss):
    sources = len(us)
    tr = us[0].shape[0]
    wide, width = down.shape
    return pl.pallas_call(
        functools.partial(down_body, sources, rank),
        in_specs=[VM] * (sources + 2),
        out_specs=VM,
        out_shape=jax.ShapeDtypeStruct((rank + EXT, sources * tr), BF),
        scratch_shapes=[pltpu.VMEM((sources * tr, width), BF)],
        compiler_params=params(20),
        cost_estimate=pl.CostEstimate(
            flops=2 * sources * tr * wide * width, bytes_accessed=2 * wide * width, transcendentals=0
        ),
        name="adapter_down",
    )(*us, down, ss)


def up_body(rank, width, own_ref, pair_ref, other_ref, up_ref, here_ref, near_ref, far_ref, both_ref, scale_ref):
    tr = here_ref.shape[0]
    wide = up_ref.shape[0]
    lanes = own_ref.shape[1]
    slots = own_ref[rank:].astype(F32)[:1]
    total = pair_ref[:rank].astype(F32) + other_ref[:rank].astype(F32)
    tail = pair_ref[rank:].astype(F32) + other_ref[rank:].astype(F32)
    tail = tail[:, :LANES]
    squares = (tail[1:2] + tail[2:3]) + (tail[3:4] + tail[4:5])
    scale = jnp.broadcast_to(lax.rsqrt(squares / width + EPSILON), (8, LANES)).T
    scale_ref[...] = jnp.broadcast_to(scale[:tr, :1], (tr, LANES))
    first = lax.axis_index("dp") * (wide // rank)
    cell = (lax.broadcasted_iota(jnp.int32, (lanes, wide), 1) // rank + first).astype(F32)
    twice = jnp.concatenate([total] * (LANES // rank), axis=0).T.astype(BF).astype(F32)
    slot = jnp.broadcast_to(slots, (8, lanes)).T[:, :1]
    spread = jnp.concatenate([twice] * (wide // LANES), axis=1)
    rows = jnp.where(cell == slot, spread, 0.0).astype(BF)
    delta = dot(rows, up_ref[...])
    here_ref[...] = delta[:tr].astype(BF)
    near_ref[...] = delta[tr : 2 * tr].astype(BF)
    far_ref[...] = delta[2 * tr : 3 * tr].astype(BF)
    both_ref[...] = delta[3 * tr :].astype(BF)


def up_call(own, pair, other, up, rank, width, tr):
    lanes = own.shape[1]
    wide, features = up.shape
    return pl.pallas_call(
        functools.partial(up_body, rank, width),
        in_specs=[VM] * 4,
        out_specs=[VM] * 5,
        out_shape=[
            jax.ShapeDtypeStruct((tr, features), BF),
            jax.ShapeDtypeStruct((tr, features), BF),
            jax.ShapeDtypeStruct((tr, features), BF),
            jax.ShapeDtypeStruct((tr, features), BF),
            jax.ShapeDtypeStruct((tr, LANES), F32),
        ],
        compiler_params=params(16),
        cost_estimate=pl.CostEstimate(
            flops=2 * lanes * wide * features, bytes_accessed=2 * wide * features, transcendentals=0
        ),
        name="adapter_up",
    )(own, pair, other, up)


def sum_body(own_ref, mid_ref, here_ref, side_ref, out_ref):
    total = own_ref[...] + mid_ref[...].astype(F32)
    out_ref[...] = total + here_ref[...].astype(F32) + side_ref[...].astype(F32)


def sum_call(own, mid, here, side):
    return pl.pallas_call(
        sum_body,
        in_specs=[VM] * 4,
        out_specs=VM,
        out_shape=jax.ShapeDtypeStruct(own.shape, F32),
        compiler_params=params(8),
        cost_estimate=pl.CostEstimate(flops=4 * own.size, bytes_accessed=2000000, transcendentals=0),
        name="sum_parts",
    )(own, mid, here, side)


def swap(a, axis, size, bit):
    return lax.ppermute(a, axis, [(i, i ^ bit) for i in range(size)])


def after(a, *others):
    return lax.optimization_barrier((a,) + others)[0]


def per_device_pairs(
    dp,
    tensor,
    row_adapter_index,
    adapter_storage_row,
    initial_head_state,
    step_head_input,
    step_gate_input,
    step_size_logits,
    state_write_key,
    state_read_query,
    head_decay_rate,
    head_skip_gain,
    gated_norm_gain,
    output_weight,
    adapter_down_weight,
    adapter_up_weight,
):
    steps, rows, width = step_head_input.shape
    tr = steps * rows
    stored, _, rank = adapter_down_weight.shape
    features = adapter_up_weight.shape[2]
    down = jnp.swapaxes(adapter_down_weight, 1, 2).reshape(stored * rank, width)
    up = adapter_up_weight.reshape(stored * rank, features)
    weight = hbm(output_weight)
    state_args = (
        hbm(row_adapter_index),
        hbm(adapter_storage_row),
        hbm(initial_head_state),
        hbm(step_head_input),
        hbm(step_gate_input),
        hbm(step_size_logits),
        hbm(state_write_key),
        hbm(state_read_query),
        hbm(head_decay_rate[None]),
        hbm(head_skip_gain[None]),
        hbm(gated_norm_gain[None]),
    )
    carried, u, ss = state_call(state_args, 8)
    far_u = swap(u, "dp", dp, 2)
    near_u = swap(u, "dp", dp, 1)
    (far,) = base_call(u, weight, (3,), [BF], features, "base_first")
    near_in = swap(far, "tensor", tensor, 1)
    mid, near, own = base_call(after(u, far), weight, (2, 1, 0), [F32, BF, F32], features, "base_rest")
    both_u = swap(after(far_u, own), "dp", dp, 1)
    near_own = swap(near, "tensor", tensor, 1)
    mid = (mid + near_in.astype(F32)).astype(BF)
    mid_in = swap(mid, "tensor", tensor, 2)
    msg = down_call([after(u, mid), near_u, far_u, both_u], down, rank, ss)
    pair = (msg.astype(F32) + swap(msg, "tensor", tensor, 1).astype(F32)).astype(BF)
    other = swap(pair, "tensor", tensor, 2)
    here, side, over, both, scale = up_call(after(msg, near_own), pair, other, up, rank, width * tensor, tr)
    both_in = swap(both, "dp", dp, 1)
    side_in = swap(side, "dp", dp, 1)
    over_in = swap(over + both_in, "dp", dp, 2)
    half = sum_call(own, mid_in, here, side_in)
    mixed_out = ((half + near_own.astype(F32) + over_in.astype(F32)) * scale[:, :1]).astype(BF).reshape(steps, rows, features)
    return mixed_out, carried


def slot_lookup(row_adapter_index, adapter_storage_row):
    match = row_adapter_index[:, None] == lax.broadcasted_iota(
        jnp.int32, (row_adapter_index.shape[0], adapter_storage_row.shape[0]), 1
    )
    return jnp.sum(jnp.where(match, adapter_storage_row[None, :], 0), axis=1)


def per_device_any(
    row_adapter_index,
    adapter_storage_row,
    initial_head_state,
    step_head_input,
    step_gate_input,
    step_size_logits,
    state_write_key,
    state_read_query,
    head_decay_rate,
    head_skip_gain,
    gated_norm_gain,
    output_weight,
    adapter_down_weight,
    adapter_up_weight,
):
    steps_n, row_count, width = step_head_input.shape
    head_count = head_decay_rate.shape[0]
    head_dim = width // head_count
    carried = initial_head_state
    gated_list = []
    for moment in range(steps_n):
        delta_t = jax.nn.softplus(step_size_logits[moment])
        damping = jnp.exp(-delta_t * head_decay_rate[None, :])
        values = (
            step_head_input[moment].astype(jnp.float32).reshape(row_count, head_count, head_dim)
        )
        writer = state_write_key[moment].astype(jnp.float32)
        reader = state_read_query[moment].astype(jnp.float32)
        updated = (
            damping[:, :, None, None] * carried.astype(jnp.float32)
            + (delta_t[:, :, None] * values)[:, :, :, None] * writer[:, None, None, :]
        )
        carried = updated.astype(jnp.bfloat16)
        output = (
            jnp.sum(updated * reader[:, None, None, :], axis=3)
            + head_skip_gain[None, :, None] * values
        )
        gated_list.append(
            output.reshape(row_count, width)
            * jax.nn.silu(step_gate_input[moment].astype(jnp.float32))
        )
    gated_all = jnp.stack(gated_list)
    totals = lax.psum(jnp.sum(gated_all * gated_all, axis=2), "tensor")
    scaling = lax.rsqrt(totals / (STATE_HEADS * HEAD_WIDTH) + EPSILON)
    normed = (gated_all * scaling[:, :, None] * gated_norm_gain[None, None, :]).astype(jnp.bfloat16)
    base = jnp.dot(
        normed.reshape(steps_n * row_count, width),
        output_weight,
        preferred_element_type=jnp.float32,
    )
    base = lax.psum_scatter(
        base.reshape(steps_n, row_count, -1), "tensor", scatter_dimension=2, tiled=True
    )
    running_state = adapter_down_weight.shape[0]
    slots = slot_lookup(row_adapter_index, adapter_storage_row)
    columns = lax.broadcasted_iota(jnp.int32, (row_count, adapter_storage_row.shape[0]), 1)
    marks = (slots[:, None] == columns).astype(jnp.bfloat16)
    normed_steps_list, every_mark = (
        lax.all_gather(normed, "dp", axis=1, tiled=True),
        lax.all_gather(marks, "dp", axis=0, tiled=True),
    )
    owned = lax.dynamic_slice_in_dim(
        every_mark, lax.axis_index("dp") * running_state, running_state, 1
    )
    partial_down = jnp.einsum(
        "pcu,oue->pcoe", normed_steps_list, adapter_down_weight, preferred_element_type=jnp.float32
    )
    picked = jnp.sum(partial_down * owned.astype(jnp.float32)[None, :, :, None], axis=2)
    down_projected = lax.psum(picked, "tensor").astype(jnp.bfloat16)
    up_projected = down_projected[:, :, None, :] * owned[None, :, :, None]
    adapter_delta = jnp.einsum(
        "bcuo,uoz->bcz", up_projected, adapter_up_weight, preferred_element_type=jnp.float32
    )
    adapter_delta = lax.psum_scatter(adapter_delta, "dp", scatter_dimension=1, tiled=True)
    mixed_out = (base + adapter_delta).astype(jnp.bfloat16)
    return (mixed_out, carried)


def solution(mesh):
    placed = (
        P(("groups", "dp")),
        P(),
        P(("groups", "dp"), "tensor", None, None),
        P(None, ("groups", "dp"), "tensor"),
        P(None, ("groups", "dp"), "tensor"),
        P(None, ("groups", "dp"), "tensor"),
        P(None, ("groups", "dp"), None),
        P(None, ("groups", "dp"), None),
        P("tensor"),
        P("tensor"),
        P("tensor"),
        P("tensor", None),
        P("dp", "tensor", None),
        P("dp", None, "tensor"),
    )
    dp, tensor = mesh.shape["dp"], mesh.shape["tensor"]
    body = per_device_any
    if dp == 4 and tensor == 4:
        body = functools.partial(per_device_pairs, dp, tensor)
    return jax.shard_map(
        body,
        mesh=mesh,
        in_specs=placed,
        out_specs=(P(None, ("groups", "dp"), "tensor"), P(("groups", "dp"), "tensor", None, None)),
        check_vma=False,
    )
```

```python
import functools

import jax
import jax.numpy as jnp
from jax import lax
from jax.experimental import pallas as pl
from jax.experimental.pallas import tpu as pltpu
from jax.sharding import PartitionSpec as P

STATE_HEADS = 128
HEAD_WIDTH = 64
EPSILON = 1e-05

BF = jnp.bfloat16
F32 = jnp.float32
NT = (((1,), (1,)), ((), ()))
NN = (((1,), (0,)), ((), ()))
LANES = 128
EXT = 16
MIB = 1024 * 1024

VM = pl.BlockSpec(memory_space=pltpu.VMEM)
ANY = pl.BlockSpec(memory_space=pl.ANY)


def dot(a, b, dims=NN):
    return lax.dot_general(a, b, dims, preferred_element_type=F32)


def hbm(a):
    return pltpu.with_memory_space_constraint(a, pltpu.HBM)


def params(mib):
    return pltpu.CompilerParams(vmem_limit_bytes=mib * MIB)


def state_body(hb, *refs):
    small_src = refs[:8]
    s_ref, idx_ref, store_ref = refs[8:11]
    ns_ref, u_ref, ss_ref = refs[11:14]
    x_ref, g_ref, lg_ref, rate_ref, skip_ref, gain_ref, w_ref, q_ref = refs[14:22]
    s_buf, o_buf, chi_ref, clo_ref, wbd_ref, qbd_ref, k4_ref, xet_ref, z_ref, sq_ref = refs[22:32]
    small_sem, in_sem, out_sem, idx_buf, store_buf = refs[32:]
    steps, rows, width = x_ref.shape
    heads = lg_ref.shape[2]
    n = w_ref.shape[2]
    tr = steps * rows
    cols = hb * HEAD_WIDTH
    pairs = rows // 2
    chunks = heads // hb

    def state_in(c):
        return pltpu.make_async_copy(
            s_ref.at[:, pl.ds(c * hb, hb)], s_buf.at[:, pl.ds(c * hb, hb)], in_sem.at[c]
        )

    def state_out(c):
        return pltpu.make_async_copy(
            o_buf.at[:, pl.ds(c * hb, hb)], ns_ref.at[:, pl.ds(c * hb, hb)], out_sem.at[c]
        )

    small_dst = [x_ref, g_ref, lg_ref, rate_ref, skip_ref, gain_ref, w_ref, q_ref, idx_buf, store_buf]
    small_src = list(small_src) + [idx_ref, store_ref]
    copies = [
        pltpu.make_async_copy(a, b, small_sem.at[i]) for i, (a, b) in enumerate(zip(small_src, small_dst))
    ]
    for i in (2, 3, 4, 6, 7, 0):
        copies[i].start()
    state_in(0).start()
    for i in (1, 5, 8, 9):
        copies[i].start()
    for c in range(1, chunks):
        state_in(c).start()
    for i in (2, 3, 4, 6, 7):
        copies[i].wait()

    delta = [jax.nn.softplus(lg_ref[t]) for t in range(steps)]
    keep = [jnp.exp(-delta[t] * rate_ref[...]) for t in range(steps)]
    w = [w_ref[t].astype(F32) for t in range(steps)]
    q = [q_ref[t].astype(F32) for t in range(steps)]
    cum = []
    for t in range(steps):
        cum.append(keep[t] if t == 0 else cum[-1] * keep[t])
    coef = list(cum)
    cur = []
    for t in range(steps):
        cur = [v * keep[t] for v in cur] + [delta[t]]
        for s in range(t + 1):
            a = cur[s] * jnp.sum(w[s] * q[t], axis=1, keepdims=True)
            if s == t:
                a = a + skip_ref[...]
            coef.append(a)
    coef = jnp.concatenate(cur + coef, axis=0)
    hi = coef.astype(BF)
    chi_ref[...] = hi
    clo_ref[...] = (coef - hi.astype(F32)).astype(BF)
    eye = lax.broadcasted_iota(jnp.int32, (heads, heads), 0) == lax.broadcasted_iota(
        jnp.int32, (heads, heads), 1
    )
    for r in range(rows):
        col = jnp.sum(jnp.where(eye, cum[-1][r : r + 1, :], 0.0), axis=1, keepdims=True)
        k4_ref[r] = jnp.broadcast_to(col, (heads, LANES))
    wf = jnp.concatenate(w, axis=0)
    qf = jnp.concatenate(q, axis=0)
    owner = lax.rem(lax.broadcasted_iota(jnp.int32, (tr, n), 0), rows)
    for p in range(pairs):
        for half in range(2):
            mine = owner == 2 * p + half
            wbd_ref[p, :, half * n : (half + 1) * n] = jnp.where(mine, wf, 0.0).astype(BF)
            qbd_ref[p, :, half * n : (half + 1) * n] = jnp.where(mine, qf, 0.0).astype(BF)

    hsel = lax.broadcasted_iota(jnp.int32, (heads, cols), 0)
    hcol = lax.broadcasted_iota(jnp.int32, (heads, cols), 1) // HEAD_WIDTH

    def spread(c, at):
        expand = jnp.where(hsel == hcol + c * hb, 1.0, 0.0).astype(BF)
        return dot(chi_ref[at], expand) + dot(clo_ref[at], expand)

    def columns(c):
        return pl.ds(pl.multiple_of(c * cols, cols), cols)

    def inputs(c):
        return [x_ref[t, :, columns(c)].astype(F32) for t in range(steps)]

    def scaled_inputs(c):
        e = spread(c, slice(0, tr))
        x = inputs(c)
        xe = jnp.concatenate([e[s * rows : (s + 1) * rows] * x[s] for s in range(steps)], axis=0)
        xet_ref[lax.rem(c, 2)] = xe.T.astype(BF)

    def gated_rows(c):
        z = z_ref[lax.rem(c, 2)]
        ce = spread(c, slice(tr, None))
        x = inputs(c)
        gain = gain_ref[:, columns(c)]
        at = tr
        out_rows = []
        for t in range(steps):
            y = ce[t * rows : (t + 1) * rows] * z[t * rows : (t + 1) * rows]
            for s in range(t + 1):
                y = y + ce[at : at + rows] * x[s]
                at += rows
            g = g_ref[t, :, columns(c)].astype(F32)
            gated = y * (g / (1.0 + jnp.exp(-g)))
            sq = gated * gated
            part = sq[:, :LANES]
            for b in range(1, cols // LANES):
                part = part + sq[:, b * LANES : (b + 1) * LANES]
            sq_ref[c, t * rows : (t + 1) * rows, :] = part
            out_rows.append(gated * gain)
        u_ref[:, columns(c)] = jnp.concatenate(out_rows, axis=0).astype(BF)

    copies[0].wait()
    scaled_inputs(0)
    for i in (1, 5, 8, 9):
        copies[i].wait()
    z_ref[...] = jnp.zeros_like(z_ref)

    def chunk(c, carry):
        state_in(c).wait()
        xet = xet_ref[lax.rem(c, 2)]
        z = jnp.zeros((cols, tr), F32)
        for p in range(pairs):
            s0 = s_buf[2 * p, pl.ds(c * hb, hb)].reshape(cols, n)
            s1 = s_buf[2 * p + 1, pl.ds(c * hb, hb)].reshape(cols, n)
            z = z + dot(jnp.concatenate([s0, s1], axis=1), qbd_ref[p], NT)
            up = dot(xet, wbd_ref[p])
            for half, sv in ((0, s0), (1, s1)):
                r = 2 * p + half
                k4 = k4_ref[r, pl.ds(c * hb, hb), :]
                grown = (
                    k4[:, None, :] * sv.astype(F32).reshape(hb, HEAD_WIDTH, n)
                    + up[:, half * n : (half + 1) * n].reshape(hb, HEAD_WIDTH, n)
                )
                o_buf[r, pl.ds(c * hb, hb)] = grown.astype(BF)
        scaled_inputs(jnp.minimum(c + 1, chunks - 1))
        gated_rows(jnp.maximum(c - 1, 0))
        z_ref[lax.rem(c, 2)] = z.T
        state_out(c).start()
        return carry

    lax.fori_loop(0, chunks, chunk, 0)
    gated_rows(chunks - 1)
    total = sq_ref[0]
    for c in range(1, chunks):
        total = total + sq_ref[c]
    ss_ref[...] = total
    which = lax.rem(lax.broadcasted_iota(jnp.int32, (tr, LANES), 0), rows)
    slots = jnp.zeros((tr, LANES), F32)
    for r in range(rows):
        slots = jnp.where(which == r, store_buf[idx_buf[r]].astype(F32), slots)
    u_ref[:, width:] = slots.astype(BF)
    for c in range(chunks):
        state_out(c).wait()


def state_call(args, hb):
    (idx, store, state, x, g, lg, w, q, rate, skip, gain) = args
    steps, rows, width = x.shape
    heads = rate.shape[1]
    tr = steps * rows
    n = w.shape[2]
    cols = hb * HEAD_WIDTH
    chunks = heads // hb
    operands = [x, g, lg, rate, skip, gain, w, q, state, idx, store]
    coef_rows = (steps * (steps + 1) // 2 + 2 * steps) * rows
    scratch = [
        pltpu.VMEM(x.shape, BF),
        pltpu.VMEM(g.shape, BF),
        pltpu.VMEM(lg.shape, F32),
        pltpu.VMEM(rate.shape, F32),
        pltpu.VMEM(skip.shape, F32),
        pltpu.VMEM(gain.shape, F32),
        pltpu.VMEM(w.shape, BF),
        pltpu.VMEM(q.shape, BF),
        pltpu.VMEM(state.shape, BF),
        pltpu.VMEM(state.shape, BF),
        pltpu.VMEM((coef_rows, heads), BF),
        pltpu.VMEM((coef_rows, heads), BF),
        pltpu.VMEM((rows // 2, tr, 2 * n), BF),
        pltpu.VMEM((rows // 2, tr, 2 * n), BF),
        pltpu.VMEM((rows, heads, LANES), F32),
        pltpu.VMEM((2, cols, tr), BF),
        pltpu.VMEM((2, tr, cols), F32),
        pltpu.VMEM((chunks, tr, LANES), F32),
        pltpu.SemaphoreType.DMA((10,)),
        pltpu.SemaphoreType.DMA((chunks,)),
        pltpu.SemaphoreType.DMA((chunks,)),
        pltpu.SMEM(idx.shape, jnp.int32),
        pltpu.SMEM(store.shape, jnp.int32),
    ]
    return pl.pallas_call(
        functools.partial(state_body, hb),
        in_specs=[ANY] * len(operands),
        out_specs=[ANY, VM, VM],
        out_shape=[
            jax.ShapeDtypeStruct(state.shape, BF),
            jax.ShapeDtypeStruct((tr, width + LANES), BF),
            jax.ShapeDtypeStruct((tr, LANES), F32),
        ],
        scratch_shapes=scratch,
        compiler_params=params(36),
        cost_estimate=pl.CostEstimate(
            flops=4 * tr * rows * heads * HEAD_WIDTH * n, bytes_accessed=4 * state.size, transcendentals=0
        ),
        name="state_steps",
    )(*operands)


def base_body(flips, features, u_ref, w_ref, *refs):
    outs = refs[: len(flips)]
    buf, acc, sems = refs[len(flips) :]
    pieces = buf.shape[1]
    depth = buf.shape[2]
    me = lax.axis_index("tensor")

    def fetch(k, i):
        at = pl.multiple_of((me ^ flips[k]) * features, LANES)
        return pltpu.make_async_copy(
            w_ref.at[pl.ds(i * depth, depth), pl.ds(at, features)], buf.at[k, i], sems.at[k, i]
        )

    for k in range(len(flips)):
        for i in range(pieces):
            fetch(k, i).start()
    for k in range(len(flips)):
        for i in range(pieces):
            fetch(k, i).wait()
            tile = dot(u_ref[:, i * depth : (i + 1) * depth], buf[k, i])
            if i == 0:
                acc[...] = tile
            elif i < pieces - 1:
                acc[...] += tile
            else:
                outs[k][...] = (acc[...] + tile).astype(outs[k].dtype)


def base_call(u, weight, flips, types, features, name):
    tr = u.shape[0]
    depth = weight.shape[0]
    pieces = 4
    count = len(flips)
    return pl.pallas_call(
        functools.partial(base_body, flips, features),
        in_specs=[VM, ANY],
        out_specs=[VM] * count,
        out_shape=[jax.ShapeDtypeStruct((tr, features), t) for t in types],
        scratch_shapes=[
            pltpu.VMEM((count, pieces, depth // pieces, features), BF),
            pltpu.VMEM((tr, features), F32),
            pltpu.SemaphoreType.DMA((count, pieces)),
        ],
        compiler_params=params(20),
        cost_estimate=pl.CostEstimate(
            flops=2 * tr * depth * features * count,
            bytes_accessed=2 * depth * features * count,
            transcendentals=0,
        ),
        name=name,
    )(u, weight)


def down_body(sources, rank, *refs):
    us = refs[:sources]
    down_ref, ss_ref, out_ref, rows_ref = refs[sources:]
    tr = us[0].shape[0]
    wide, width = down_ref.shape
    lanes = sources * tr
    first = lax.axis_index("dp") * (wide // rank)
    slots = []
    for k in range(sources):
        rows_ref[k * tr : (k + 1) * tr] = us[k][:, :width]
        slots.append(us[k][:, width:].astype(F32))
    slots = jnp.concatenate(slots, axis=0).T[:1]
    cell = lax.broadcasted_iota(jnp.int32, (wide, lanes), 0) // rank + first
    part = dot(down_ref[...], rows_ref[...], NT)
    part = jnp.where(cell.astype(F32) == slots, part, 0.0)
    total = part[:rank]
    for a in range(1, wide // rank):
        total = total + part[a * rank : (a + 1) * rank]
    ss = jnp.sum(ss_ref[...].T, axis=0, keepdims=True)
    hi = ss.astype(BF).astype(F32)
    gap = jnp.zeros((1, lanes - tr), F32)
    row = lax.broadcasted_iota(jnp.int32, (EXT, lanes), 0)
    at = 1 + 2 * lax.rem(lax.axis_index("tensor"), 2)
    tail = jnp.where(row == 0, slots, 0.0)
    tail = jnp.where(row == at, jnp.concatenate([hi, gap], axis=1), tail)
    tail = jnp.where(row == at + 1, jnp.concatenate([ss - hi, gap], axis=1), tail)
    out_ref[:rank] = total.astype(BF)
    out_ref[rank:] = tail.astype(BF)


def down_call(us, down, rank, ss):
    sources = len(us)
    tr = us[0].shape[0]
    wide, width = down.shape
    return pl.pallas_call(
        functools.partial(down_body, sources, rank),
        in_specs=[VM] * (sources + 2),
        out_specs=VM,
        out_shape=jax.ShapeDtypeStruct((rank + EXT, sources * tr), BF),
        scratch_shapes=[pltpu.VMEM((sources * tr, width), BF)],
        compiler_params=params(20),
        cost_estimate=pl.CostEstimate(
            flops=2 * sources * tr * wide * width, bytes_accessed=2 * wide * width, transcendentals=0
        ),
        name="adapter_down",
    )(*us, down, ss)


def up_body(rank, width, own_ref, pair_ref, other_ref, up_ref, here_ref, near_ref, far_ref, both_ref, scale_ref):
    tr = here_ref.shape[0]
    wide = up_ref.shape[0]
    lanes = own_ref.shape[1]
    slots = own_ref[rank:].astype(F32)[:1]
    total = pair_ref[:rank].astype(F32) + other_ref[:rank].astype(F32)
    tail = pair_ref[rank:].astype(F32) + other_ref[rank:].astype(F32)
    tail = tail[:, :LANES]
    squares = (tail[1:2] + tail[2:3]) + (tail[3:4] + tail[4:5])
    scale = jnp.broadcast_to(lax.rsqrt(squares / width + EPSILON), (8, LANES)).T
    scale_ref[...] = jnp.broadcast_to(scale[:tr, :1], (tr, LANES))
    first = lax.axis_index("dp") * (wide // rank)
    cell = (lax.broadcasted_iota(jnp.int32, (lanes, wide), 1) // rank + first).astype(F32)
    twice = jnp.concatenate([total] * (LANES // rank), axis=0).T.astype(BF).astype(F32)
    slot = jnp.broadcast_to(slots, (8, lanes)).T[:, :1]
    spread = jnp.concatenate([twice] * (wide // LANES), axis=1)
    rows = jnp.where(cell == slot, spread, 0.0).astype(BF)
    delta = dot(rows, up_ref[...])
    here_ref[...] = delta[:tr].astype(BF)
    near_ref[...] = delta[tr : 2 * tr].astype(BF)
    far_ref[...] = delta[2 * tr : 3 * tr].astype(BF)
    both_ref[...] = delta[3 * tr :].astype(BF)


def up_call(own, pair, other, up, rank, width, tr):
    lanes = own.shape[1]
    wide, features = up.shape
    return pl.pallas_call(
        functools.partial(up_body, rank, width),
        in_specs=[VM] * 4,
        out_specs=[VM] * 5,
        out_shape=[
            jax.ShapeDtypeStruct((tr, features), BF),
            jax.ShapeDtypeStruct((tr, features), BF),
            jax.ShapeDtypeStruct((tr, features), BF),
            jax.ShapeDtypeStruct((tr, features), BF),
            jax.ShapeDtypeStruct((tr, LANES), F32),
        ],
        compiler_params=params(16),
        cost_estimate=pl.CostEstimate(
            flops=2 * lanes * wide * features, bytes_accessed=2 * wide * features, transcendentals=0
        ),
        name="adapter_up",
    )(own, pair, other, up)


def sum_body(own_ref, mid_ref, here_ref, side_ref, out_ref):
    total = own_ref[...] + mid_ref[...].astype(F32)
    out_ref[...] = total + here_ref[...].astype(F32) + side_ref[...].astype(F32)


def sum_call(own, mid, here, side):
    return pl.pallas_call(
        sum_body,
        in_specs=[VM] * 4,
        out_specs=VM,
        out_shape=jax.ShapeDtypeStruct(own.shape, F32),
        compiler_params=params(8),
        cost_estimate=pl.CostEstimate(flops=4 * own.size, bytes_accessed=2000000, transcendentals=0),
        name="sum_parts",
    )(own, mid, here, side)


def swap(a, axis, size, bit):
    return lax.ppermute(a, axis, [(i, i ^ bit) for i in range(size)])


def after(a, *others):
    return lax.optimization_barrier((a,) + others)[0]


def per_device_pairs(
    dp,
    tensor,
    row_adapter_index,
    adapter_storage_row,
    initial_head_state,
    step_head_input,
    step_gate_input,
    step_size_logits,
    state_write_key,
    state_read_query,
    head_decay_rate,
    head_skip_gain,
    gated_norm_gain,
    output_weight,
    adapter_down_weight,
    adapter_up_weight,
):
    steps, rows, width = step_head_input.shape
    tr = steps * rows
    stored, _, rank = adapter_down_weight.shape
    features = adapter_up_weight.shape[2]
    down = jnp.swapaxes(adapter_down_weight, 1, 2).reshape(stored * rank, width)
    up = adapter_up_weight.reshape(stored * rank, features)
    weight = hbm(output_weight)
    state_args = (
        hbm(row_adapter_index),
        hbm(adapter_storage_row),
        hbm(initial_head_state),
        hbm(step_head_input),
        hbm(step_gate_input),
        hbm(step_size_logits),
        hbm(state_write_key),
        hbm(state_read_query),
        hbm(head_decay_rate[None]),
        hbm(head_skip_gain[None]),
        hbm(gated_norm_gain[None]),
    )
    carried, u, ss = state_call(state_args, 8)
    far_u = swap(u, "dp", dp, 2)
    near_u = swap(u, "dp", dp, 1)
    (far,) = base_call(u, weight, (3,), [BF], features, "base_first")
    near_in = swap(far, "tensor", tensor, 1)
    mid, near, own = base_call(after(u, far), weight, (2, 1, 0), [F32, BF, F32], features, "base_rest")
    both_u = swap(after(far_u, own), "dp", dp, 1)
    near_own = swap(near, "tensor", tensor, 1)
    mid = (mid + near_in.astype(F32)).astype(BF)
    mid_in = swap(mid, "tensor", tensor, 2)
    msg = down_call([after(u, mid), near_u, far_u, both_u], down, rank, ss)
    pair = (msg.astype(F32) + swap(msg, "tensor", tensor, 1).astype(F32)).astype(BF)
    other = swap(pair, "tensor", tensor, 2)
    here, side, over, both, scale = up_call(after(msg, near_own), pair, other, up, rank, width * tensor, tr)
    both_in = swap(both, "dp", dp, 1)
    side_in = swap(side, "dp", dp, 1)
    over_in = swap(over + both_in, "dp", dp, 2)
    half = sum_call(own, mid_in, here, side_in)
    mixed_out = ((half + near_own.astype(F32) + over_in.astype(F32)) * scale[:, :1]).astype(BF).reshape(steps, rows, features)
    return mixed_out, carried


def slot_lookup(row_adapter_index, adapter_storage_row):
    match = row_adapter_index[:, None] == lax.broadcasted_iota(
        jnp.int32, (row_adapter_index.shape[0], adapter_storage_row.shape[0]), 1
    )
    return jnp.sum(jnp.where(match, adapter_storage_row[None, :], 0), axis=1)


def per_device_any(
    row_adapter_index,
    adapter_storage_row,
    initial_head_state,
    step_head_input,
    step_gate_input,
    step_size_logits,
    state_write_key,
    state_read_query,
    head_decay_rate,
    head_skip_gain,
    gated_norm_gain,
    output_weight,
    adapter_down_weight,
    adapter_up_weight,
):
    steps_n, row_count, width = step_head_input.shape
    head_count = head_decay_rate.shape[0]
    head_dim = width // head_count
    carried = initial_head_state
    gated_list = []
    for moment in range(steps_n):
        delta_t = jax.nn.softplus(step_size_logits[moment])
        damping = jnp.exp(-delta_t * head_decay_rate[None, :])
        values = (
            step_head_input[moment].astype(jnp.float32).reshape(row_count, head_count, head_dim)
        )
        writer = state_write_key[moment].astype(jnp.float32)
        reader = state_read_query[moment].astype(jnp.float32)
        updated = (
            damping[:, :, None, None] * carried.astype(jnp.float32)
            + (delta_t[:, :, None] * values)[:, :, :, None] * writer[:, None, None, :]
        )
        carried = updated.astype(jnp.bfloat16)
        output = (
            jnp.sum(updated * reader[:, None, None, :], axis=3)
            + head_skip_gain[None, :, None] * values
        )
        gated_list.append(
            output.reshape(row_count, width)
            * jax.nn.silu(step_gate_input[moment].astype(jnp.float32))
        )
    gated_all = jnp.stack(gated_list)
    totals = lax.psum(jnp.sum(gated_all * gated_all, axis=2), "tensor")
    scaling = lax.rsqrt(totals / (STATE_HEADS * HEAD_WIDTH) + EPSILON)
    normed = (gated_all * scaling[:, :, None] * gated_norm_gain[None, None, :]).astype(jnp.bfloat16)
    base = jnp.dot(
        normed.reshape(steps_n * row_count, width),
        output_weight,
        preferred_element_type=jnp.float32,
    )
    base = lax.psum_scatter(
        base.reshape(steps_n, row_count, -1), "tensor", scatter_dimension=2, tiled=True
    )
    running_state = adapter_down_weight.shape[0]
    slots = slot_lookup(row_adapter_index, adapter_storage_row)
    columns = lax.broadcasted_iota(jnp.int32, (row_count, adapter_storage_row.shape[0]), 1)
    marks = (slots[:, None] == columns).astype(jnp.bfloat16)
    normed_steps_list, every_mark = (
        lax.all_gather(normed, "dp", axis=1, tiled=True),
        lax.all_gather(marks, "dp", axis=0, tiled=True),
    )
    owned = lax.dynamic_slice_in_dim(
        every_mark, lax.axis_index("dp") * running_state, running_state, 1
    )
    partial_down = jnp.einsum(
        "pcu,oue->pcoe", normed_steps_list, adapter_down_weight, preferred_element_type=jnp.float32
    )
    picked = jnp.sum(partial_down * owned.astype(jnp.float32)[None, :, :, None], axis=2)
    down_projected = lax.psum(picked, "tensor").astype(jnp.bfloat16)
    up_projected = down_projected[:, :, None, :] * owned[None, :, :, None]
    adapter_delta = jnp.einsum(
        "bcuo,uoz->bcz", up_projected, adapter_up_weight, preferred_element_type=jnp.float32
    )
    adapter_delta = lax.psum_scatter(adapter_delta, "dp", scatter_dimension=1, tiled=True)
    mixed_out = (base + adapter_delta).astype(jnp.bfloat16)
    return (mixed_out, carried)


def solution(mesh):
    placed = (
        P(("groups", "dp")),
        P(),
        P(("groups", "dp"), "tensor", None, None),
        P(None, ("groups", "dp"), "tensor"),
        P(None, ("groups", "dp"), "tensor"),
        P(None, ("groups", "dp"), "tensor"),
        P(None, ("groups", "dp"), None),
        P(None, ("groups", "dp"), None),
        P("tensor"),
        P("tensor"),
        P("tensor"),
        P("tensor", None),
        P("dp", "tensor", None),
        P("dp", None, "tensor"),
    )
    dp, tensor = mesh.shape["dp"], mesh.shape["tensor"]
    body = per_device_any
    if dp == 4 and tensor == 4:
        body = functools.partial(per_device_pairs, dp, tensor)
    return jax.shard_map(
        body,
        mesh=mesh,
        in_specs=placed,
        out_specs=(P(None, ("groups", "dp"), "tensor"), P(("groups", "dp"), "tensor", None, None)),
        check_vma=False,
    )
```

```python
import functools

import jax
import jax.numpy as jnp
from jax import lax
from jax.experimental import pallas as pl
from jax.experimental.pallas import tpu as pltpu
from jax.sharding import PartitionSpec as P

STATE_HEADS = 128
HEAD_WIDTH = 64
EPSILON = 1e-05

BF = jnp.bfloat16
F32 = jnp.float32
NT = (((1,), (1,)), ((), ()))
NN = (((1,), (0,)), ((), ()))
LANES = 128
EXT = 16
MIB = 1024 * 1024

VM = pl.BlockSpec(memory_space=pltpu.VMEM)
ANY = pl.BlockSpec(memory_space=pl.ANY)


def dot(a, b, dims=NN):
    return lax.dot_general(a, b, dims, preferred_element_type=F32)


def hbm(a):
    return pltpu.with_memory_space_constraint(a, pltpu.HBM)


def params(mib):
    return pltpu.CompilerParams(vmem_limit_bytes=mib * MIB)


def state_body(hb, *refs):
    small_src = refs[:8]
    s_ref, idx_ref, store_ref = refs[8:11]
    ns_ref, u_ref, ss_ref = refs[11:14]
    x_ref, g_ref, lg_ref, rate_ref, skip_ref, gain_ref, w_ref, q_ref = refs[14:22]
    s_buf, o_buf, chi_ref, clo_ref, wbd_ref, qbd_ref, k4_ref, xet_ref, z_ref, sq_ref = refs[22:32]
    small_sem, in_sem, out_sem, idx_buf, store_buf = refs[32:]
    steps, rows, width = x_ref.shape
    heads = lg_ref.shape[2]
    n = w_ref.shape[2]
    tr = steps * rows
    cols = hb * HEAD_WIDTH
    pairs = rows // 2
    chunks = heads // hb

    def state_in(c):
        return pltpu.make_async_copy(
            s_ref.at[:, pl.ds(c * hb, hb)], s_buf.at[:, pl.ds(c * hb, hb)], in_sem.at[c]
        )

    def state_out(c):
        return pltpu.make_async_copy(
            o_buf.at[:, pl.ds(c * hb, hb)], ns_ref.at[:, pl.ds(c * hb, hb)], out_sem.at[c]
        )

    small_dst = [x_ref, g_ref, lg_ref, rate_ref, skip_ref, gain_ref, w_ref, q_ref, idx_buf, store_buf]
    small_src = list(small_src) + [idx_ref, store_ref]
    copies = [
        pltpu.make_async_copy(a, b, small_sem.at[i]) for i, (a, b) in enumerate(zip(small_src, small_dst))
    ]
    for i in (2, 3, 4, 6, 7, 0):
        copies[i].start()
    state_in(0).start()
    for i in (1, 5, 8, 9):
        copies[i].start()
    for c in range(1, chunks):
        state_in(c).start()
    for i in (2, 3, 4, 6, 7):
        copies[i].wait()

    delta = [jax.nn.softplus(lg_ref[t]) for t in range(steps)]
    keep = [jnp.exp(-delta[t] * rate_ref[...]) for t in range(steps)]
    w = [w_ref[t].astype(F32) for t in range(steps)]
    q = [q_ref[t].astype(F32) for t in range(steps)]
    cum = []
    for t in range(steps):
        cum.append(keep[t] if t == 0 else cum[-1] * keep[t])
    coef = list(cum)
    cur = []
    for t in range(steps):
        cur = [v * keep[t] for v in cur] + [delta[t]]
        for s in range(t + 1):
            a = cur[s] * jnp.sum(w[s] * q[t], axis=1, keepdims=True)
            if s == t:
                a = a + skip_ref[...]
            coef.append(a)
    coef = jnp.concatenate(cur + coef, axis=0)
    hi = coef.astype(BF)
    chi_ref[...] = hi
    clo_ref[...] = (coef - hi.astype(F32)).astype(BF)
    eye = lax.broadcasted_iota(jnp.int32, (heads, heads), 0) == lax.broadcasted_iota(
        jnp.int32, (heads, heads), 1
    )
    for r in range(rows):
        col = jnp.sum(jnp.where(eye, cum[-1][r : r + 1, :], 0.0), axis=1, keepdims=True)
        k4_ref[r] = jnp.broadcast_to(col, (heads, LANES))
    wf = jnp.concatenate(w, axis=0)
    qf = jnp.concatenate(q, axis=0)
    owner = lax.rem(lax.broadcasted_iota(jnp.int32, (tr, n), 0), rows)
    for p in range(pairs):
        for half in range(2):
            mine = owner == 2 * p + half
            wbd_ref[p, :, half * n : (half + 1) * n] = jnp.where(mine, wf, 0.0).astype(BF)
            qbd_ref[p, :, half * n : (half + 1) * n] = jnp.where(mine, qf, 0.0).astype(BF)

    hsel = lax.broadcasted_iota(jnp.int32, (heads, cols), 0)
    hcol = lax.broadcasted_iota(jnp.int32, (heads, cols), 1) // HEAD_WIDTH

    def spread(c, at):
        expand = jnp.where(hsel == hcol + c * hb, 1.0, 0.0).astype(BF)
        return dot(chi_ref[at], expand) + dot(clo_ref[at], expand)

    def columns(c):
        return pl.ds(pl.multiple_of(c * cols, cols), cols)

    def inputs(c):
        return [x_ref[t, :, columns(c)].astype(F32) for t in range(steps)]

    def scaled_inputs(c):
        e = spread(c, slice(0, tr))
        x = inputs(c)
        xe = jnp.concatenate([e[s * rows : (s + 1) * rows] * x[s] for s in range(steps)], axis=0)
        xet_ref[lax.rem(c, 2)] = xe.T.astype(BF)

    def gated_rows(c):
        z = z_ref[lax.rem(c, 2)]
        ce = spread(c, slice(tr, None))
        x = inputs(c)
        gain = gain_ref[:, columns(c)]
        at = tr
        out_rows = []
        for t in range(steps):
            y = ce[t * rows : (t + 1) * rows] * z[t * rows : (t + 1) * rows]
            for s in range(t + 1):
                y = y + ce[at : at + rows] * x[s]
                at += rows
            g = g_ref[t, :, columns(c)].astype(F32)
            gated = y * (g / (1.0 + jnp.exp(-g)))
            sq = gated * gated
            part = sq[:, :LANES]
            for b in range(1, cols // LANES):
                part = part + sq[:, b * LANES : (b + 1) * LANES]
            sq_ref[c, t * rows : (t + 1) * rows, :] = part
            out_rows.append(gated * gain)
        u_ref[:, columns(c)] = jnp.concatenate(out_rows, axis=0).astype(BF)

    copies[0].wait()
    scaled_inputs(0)
    for i in (1, 5, 8, 9):
        copies[i].wait()
    z_ref[...] = jnp.zeros_like(z_ref)

    def chunk(c, carry):
        state_in(c).wait()
        xet = xet_ref[lax.rem(c, 2)]
        z = jnp.zeros((cols, tr), F32)
        for p in range(pairs):
            s0 = s_buf[2 * p, pl.ds(c * hb, hb)].reshape(cols, n)
            s1 = s_buf[2 * p + 1, pl.ds(c * hb, hb)].reshape(cols, n)
            z = z + dot(jnp.concatenate([s0, s1], axis=1), qbd_ref[p], NT)
            up = dot(xet, wbd_ref[p])
            for half, sv in ((0, s0), (1, s1)):
                r = 2 * p + half
                k4 = k4_ref[r, pl.ds(c * hb, hb), :]
                grown = (
                    k4[:, None, :] * sv.astype(F32).reshape(hb, HEAD_WIDTH, n)
                    + up[:, half * n : (half + 1) * n].reshape(hb, HEAD_WIDTH, n)
                )
                o_buf[r, pl.ds(c * hb, hb)] = grown.astype(BF)
        state_out(c).start()
        scaled_inputs(jnp.minimum(c + 1, chunks - 1))
        gated_rows(jnp.maximum(c - 1, 0))
        z_ref[lax.rem(c, 2)] = z.T
        return carry

    lax.fori_loop(0, chunks, chunk, 0)
    gated_rows(chunks - 1)
    total = sq_ref[0]
    for c in range(1, chunks):
        total = total + sq_ref[c]
    ss_ref[...] = total
    which = lax.rem(lax.broadcasted_iota(jnp.int32, (tr, LANES), 0), rows)
    slots = jnp.zeros((tr, LANES), F32)
    for r in range(rows):
        slots = jnp.where(which == r, store_buf[idx_buf[r]].astype(F32), slots)
    u_ref[:, width:] = slots.astype(BF)
    for c in range(chunks):
        state_out(c).wait()


def state_call(args, hb):
    (idx, store, state, x, g, lg, w, q, rate, skip, gain) = args
    steps, rows, width = x.shape
    heads = rate.shape[1]
    tr = steps * rows
    n = w.shape[2]
    cols = hb * HEAD_WIDTH
    chunks = heads // hb
    operands = [x, g, lg, rate, skip, gain, w, q, state, idx, store]
    coef_rows = (steps * (steps + 1) // 2 + 2 * steps) * rows
    scratch = [
        pltpu.VMEM(x.shape, BF),
        pltpu.VMEM(g.shape, BF),
        pltpu.VMEM(lg.shape, F32),
        pltpu.VMEM(rate.shape, F32),
        pltpu.VMEM(skip.shape, F32),
        pltpu.VMEM(gain.shape, F32),
        pltpu.VMEM(w.shape, BF),
        pltpu.VMEM(q.shape, BF),
        pltpu.VMEM(state.shape, BF),
        pltpu.VMEM(state.shape, BF),
        pltpu.VMEM((coef_rows, heads), BF),
        pltpu.VMEM((coef_rows, heads), BF),
        pltpu.VMEM((rows // 2, tr, 2 * n), BF),
        pltpu.VMEM((rows // 2, tr, 2 * n), BF),
        pltpu.VMEM((rows, heads, LANES), F32),
        pltpu.VMEM((2, cols, tr), BF),
        pltpu.VMEM((2, tr, cols), F32),
        pltpu.VMEM((chunks, tr, LANES), F32),
        pltpu.SemaphoreType.DMA((10,)),
        pltpu.SemaphoreType.DMA((chunks,)),
        pltpu.SemaphoreType.DMA((chunks,)),
        pltpu.SMEM(idx.shape, jnp.int32),
        pltpu.SMEM(store.shape, jnp.int32),
    ]
    return pl.pallas_call(
        functools.partial(state_body, hb),
        in_specs=[ANY] * len(operands),
        out_specs=[ANY, VM, VM],
        out_shape=[
            jax.ShapeDtypeStruct(state.shape, BF),
            jax.ShapeDtypeStruct((tr, width + LANES), BF),
            jax.ShapeDtypeStruct((tr, LANES), F32),
        ],
        scratch_shapes=scratch,
        compiler_params=params(36),
        cost_estimate=pl.CostEstimate(
            flops=4 * tr * rows * heads * HEAD_WIDTH * n, bytes_accessed=4 * state.size, transcendentals=0
        ),
        name="state_steps",
    )(*operands)


def base_body(flips, features, u_ref, w_ref, *refs):
    outs = refs[: len(flips)]
    buf, acc, sems = refs[len(flips) :]
    pieces = buf.shape[1]
    depth = buf.shape[2]
    me = lax.axis_index("tensor")

    def fetch(k, i):
        at = pl.multiple_of((me ^ flips[k]) * features, LANES)
        return pltpu.make_async_copy(
            w_ref.at[pl.ds(i * depth, depth), pl.ds(at, features)], buf.at[k, i], sems.at[k, i]
        )

    for k in range(len(flips)):
        for i in range(pieces):
            fetch(k, i).start()
    for k in range(len(flips)):
        for i in range(pieces):
            fetch(k, i).wait()
            tile = dot(u_ref[:, i * depth : (i + 1) * depth], buf[k, i])
            if i == 0:
                acc[...] = tile
            elif i < pieces - 1:
                acc[...] += tile
            else:
                outs[k][...] = (acc[...] + tile).astype(outs[k].dtype)


def base_call(u, weight, flips, types, features, name):
    tr = u.shape[0]
    depth = weight.shape[0]
    pieces = 4
    count = len(flips)
    return pl.pallas_call(
        functools.partial(base_body, flips, features),
        in_specs=[VM, ANY],
        out_specs=[VM] * count,
        out_shape=[jax.ShapeDtypeStruct((tr, features), t) for t in types],
        scratch_shapes=[
            pltpu.VMEM((count, pieces, depth // pieces, features), BF),
            pltpu.VMEM((tr, features), F32),
            pltpu.SemaphoreType.DMA((count, pieces)),
        ],
        compiler_params=params(20),
        cost_estimate=pl.CostEstimate(
            flops=2 * tr * depth * features * count,
            bytes_accessed=2 * depth * features * count,
            transcendentals=0,
        ),
        name=name,
    )(u, weight)


def down_body(sources, rank, *refs):
    us = refs[:sources]
    down_ref, ss_ref, out_ref, rows_ref = refs[sources:]
    tr = us[0].shape[0]
    wide, width = down_ref.shape
    lanes = sources * tr
    first = lax.axis_index("dp") * (wide // rank)
    slots = []
    for k in range(sources):
        rows_ref[k * tr : (k + 1) * tr] = us[k][:, :width]
        slots.append(us[k][:, width:].astype(F32))
    slots = jnp.concatenate(slots, axis=0).T[:1]
    cell = lax.broadcasted_iota(jnp.int32, (wide, lanes), 0) // rank + first
    part = dot(down_ref[...], rows_ref[...], NT)
    part = jnp.where(cell.astype(F32) == slots, part, 0.0)
    total = part[:rank]
    for a in range(1, wide // rank):
        total = total + part[a * rank : (a + 1) * rank]
    ss = jnp.sum(ss_ref[...].T, axis=0, keepdims=True)
    hi = ss.astype(BF).astype(F32)
    gap = jnp.zeros((1, lanes - tr), F32)
    row = lax.broadcasted_iota(jnp.int32, (EXT, lanes), 0)
    at = 1 + 2 * lax.rem(lax.axis_index("tensor"), 2)
    tail = jnp.where(row == 0, slots, 0.0)
    tail = jnp.where(row == at, jnp.concatenate([hi, gap], axis=1), tail)
    tail = jnp.where(row == at + 1, jnp.concatenate([ss - hi, gap], axis=1), tail)
    out_ref[:rank] = total.astype(BF)
    out_ref[rank:] = tail.astype(BF)


def down_call(us, down, rank, ss):
    sources = len(us)
    tr = us[0].shape[0]
    wide, width = down.shape
    return pl.pallas_call(
        functools.partial(down_body, sources, rank),
        in_specs=[VM] * (sources + 2),
        out_specs=VM,
        out_shape=jax.ShapeDtypeStruct((rank + EXT, sources * tr), BF),
        scratch_shapes=[pltpu.VMEM((sources * tr, width), BF)],
        compiler_params=params(20),
        cost_estimate=pl.CostEstimate(
            flops=2 * sources * tr * wide * width, bytes_accessed=2 * wide * width, transcendentals=0
        ),
        name="adapter_down",
    )(*us, down, ss)


def up_body(rank, width, own_ref, pair_ref, other_ref, up_ref, here_ref, near_ref, far_ref, both_ref, scale_ref):
    tr = here_ref.shape[0]
    wide = up_ref.shape[0]
    lanes = own_ref.shape[1]
    slots = own_ref[rank:].astype(F32)[:1]
    total = pair_ref[:rank].astype(F32) + other_ref[:rank].astype(F32)
    tail = pair_ref[rank:].astype(F32) + other_ref[rank:].astype(F32)
    tail = tail[:, :LANES]
    squares = (tail[1:2] + tail[2:3]) + (tail[3:4] + tail[4:5])
    scale = jnp.broadcast_to(lax.rsqrt(squares / width + EPSILON), (8, LANES)).T
    scale_ref[...] = jnp.broadcast_to(scale[:tr, :1], (tr, LANES))
    first = lax.axis_index("dp") * (wide // rank)
    cell = (lax.broadcasted_iota(jnp.int32, (lanes, wide), 1) // rank + first).astype(F32)
    twice = jnp.concatenate([total] * (LANES // rank), axis=0).T.astype(BF).astype(F32)
    slot = jnp.broadcast_to(slots, (8, lanes)).T[:, :1]
    spread = jnp.concatenate([twice] * (wide // LANES), axis=1)
    rows = jnp.where(cell == slot, spread, 0.0).astype(BF)
    delta = dot(rows, up_ref[...])
    here_ref[...] = delta[:tr].astype(BF)
    near_ref[...] = delta[tr : 2 * tr].astype(BF)
    far_ref[...] = delta[2 * tr : 3 * tr].astype(BF)
    both_ref[...] = delta[3 * tr :].astype(BF)


def up_call(own, pair, other, up, rank, width, tr):
    lanes = own.shape[1]
    wide, features = up.shape
    return pl.pallas_call(
        functools.partial(up_body, rank, width),
        in_specs=[VM] * 4,
        out_specs=[VM] * 5,
        out_shape=[
            jax.ShapeDtypeStruct((tr, features), BF),
            jax.ShapeDtypeStruct((tr, features), BF),
            jax.ShapeDtypeStruct((tr, features), BF),
            jax.ShapeDtypeStruct((tr, features), BF),
            jax.ShapeDtypeStruct((tr, LANES), F32),
        ],
        compiler_params=params(16),
        cost_estimate=pl.CostEstimate(
            flops=2 * lanes * wide * features, bytes_accessed=2 * wide * features, transcendentals=0
        ),
        name="adapter_up",
    )(own, pair, other, up)


def sum_body(own_ref, mid_ref, here_ref, side_ref, out_ref):
    total = own_ref[...] + mid_ref[...].astype(F32)
    out_ref[...] = total + here_ref[...].astype(F32) + side_ref[...].astype(F32)


def sum_call(own, mid, here, side):
    return pl.pallas_call(
        sum_body,
        in_specs=[VM] * 4,
        out_specs=VM,
        out_shape=jax.ShapeDtypeStruct(own.shape, F32),
        compiler_params=params(8),
        cost_estimate=pl.CostEstimate(flops=4 * own.size, bytes_accessed=2000000, transcendentals=0),
        name="sum_parts",
    )(own, mid, here, side)


def swap(a, axis, size, bit):
    return lax.ppermute(a, axis, [(i, i ^ bit) for i in range(size)])


def after(a, *others):
    return lax.optimization_barrier((a,) + others)[0]


def per_device_pairs(
    dp,
    tensor,
    row_adapter_index,
    adapter_storage_row,
    initial_head_state,
    step_head_input,
    step_gate_input,
    step_size_logits,
    state_write_key,
    state_read_query,
    head_decay_rate,
    head_skip_gain,
    gated_norm_gain,
    output_weight,
    adapter_down_weight,
    adapter_up_weight,
):
    steps, rows, width = step_head_input.shape
    tr = steps * rows
    stored, _, rank = adapter_down_weight.shape
    features = adapter_up_weight.shape[2]
    down = jnp.swapaxes(adapter_down_weight, 1, 2).reshape(stored * rank, width)
    up = adapter_up_weight.reshape(stored * rank, features)
    weight = hbm(output_weight)
    state_args = (
        hbm(row_adapter_index),
        hbm(adapter_storage_row),
        hbm(initial_head_state),
        hbm(step_head_input),
        hbm(step_gate_input),
        hbm(step_size_logits),
        hbm(state_write_key),
        hbm(state_read_query),
        hbm(head_decay_rate[None]),
        hbm(head_skip_gain[None]),
        hbm(gated_norm_gain[None]),
    )
    carried, u, ss = state_call(state_args, 8)
    far_u = swap(u, "dp", dp, 2)
    near_u = swap(u, "dp", dp, 1)
    (far,) = base_call(u, weight, (3,), [BF], features, "base_first")
    near_in = swap(far, "tensor", tensor, 1)
    mid, near, own = base_call(after(u, far), weight, (2, 1, 0), [F32, BF, F32], features, "base_rest")
    both_u = swap(after(far_u, own), "dp", dp, 1)
    near_own = swap(near, "tensor", tensor, 1)
    mid = (mid + near_in.astype(F32)).astype(BF)
    mid_in = swap(mid, "tensor", tensor, 2)
    msg = down_call([after(u, mid), near_u, far_u, both_u], down, rank, ss)
    pair = (msg.astype(F32) + swap(msg, "tensor", tensor, 1).astype(F32)).astype(BF)
    other = swap(pair, "tensor", tensor, 2)
    here, side, over, both, scale = up_call(after(msg, near_own), pair, other, up, rank, width * tensor, tr)
    both_in = swap(both, "dp", dp, 1)
    side_in = swap(side, "dp", dp, 1)
    over_in = swap(over + both_in, "dp", dp, 2)
    half = sum_call(own, mid_in, here, side_in)
    mixed_out = ((half + near_own.astype(F32) + over_in.astype(F32)) * scale[:, :1]).astype(BF).reshape(steps, rows, features)
    return mixed_out, carried


def slot_lookup(row_adapter_index, adapter_storage_row):
    match = row_adapter_index[:, None] == lax.broadcasted_iota(
        jnp.int32, (row_adapter_index.shape[0], adapter_storage_row.shape[0]), 1
    )
    return jnp.sum(jnp.where(match, adapter_storage_row[None, :], 0), axis=1)


def per_device_any(
    row_adapter_index,
    adapter_storage_row,
    initial_head_state,
    step_head_input,
    step_gate_input,
    step_size_logits,
    state_write_key,
    state_read_query,
    head_decay_rate,
    head_skip_gain,
    gated_norm_gain,
    output_weight,
    adapter_down_weight,
    adapter_up_weight,
):
    steps_n, row_count, width = step_head_input.shape
    head_count = head_decay_rate.shape[0]
    head_dim = width // head_count
    carried = initial_head_state
    gated_list = []
    for moment in range(steps_n):
        delta_t = jax.nn.softplus(step_size_logits[moment])
        damping = jnp.exp(-delta_t * head_decay_rate[None, :])
        values = (
            step_head_input[moment].astype(jnp.float32).reshape(row_count, head_count, head_dim)
        )
        writer = state_write_key[moment].astype(jnp.float32)
        reader = state_read_query[moment].astype(jnp.float32)
        updated = (
            damping[:, :, None, None] * carried.astype(jnp.float32)
            + (delta_t[:, :, None] * values)[:, :, :, None] * writer[:, None, None, :]
        )
        carried = updated.astype(jnp.bfloat16)
        output = (
            jnp.sum(updated * reader[:, None, None, :], axis=3)
            + head_skip_gain[None, :, None] * values
        )
        gated_list.append(
            output.reshape(row_count, width)
            * jax.nn.silu(step_gate_input[moment].astype(jnp.float32))
        )
    gated_all = jnp.stack(gated_list)
    totals = lax.psum(jnp.sum(gated_all * gated_all, axis=2), "tensor")
    scaling = lax.rsqrt(totals / (STATE_HEADS * HEAD_WIDTH) + EPSILON)
    normed = (gated_all * scaling[:, :, None] * gated_norm_gain[None, None, :]).astype(jnp.bfloat16)
    base = jnp.dot(
        normed.reshape(steps_n * row_count, width),
        output_weight,
        preferred_element_type=jnp.float32,
    )
    base = lax.psum_scatter(
        base.reshape(steps_n, row_count, -1), "tensor", scatter_dimension=2, tiled=True
    )
    running_state = adapter_down_weight.shape[0]
    slots = slot_lookup(row_adapter_index, adapter_storage_row)
    columns = lax.broadcasted_iota(jnp.int32, (row_count, adapter_storage_row.shape[0]), 1)
    marks = (slots[:, None] == columns).astype(jnp.bfloat16)
    normed_steps_list, every_mark = (
        lax.all_gather(normed, "dp", axis=1, tiled=True),
        lax.all_gather(marks, "dp", axis=0, tiled=True),
    )
    owned = lax.dynamic_slice_in_dim(
        every_mark, lax.axis_index("dp") * running_state, running_state, 1
    )
    partial_down = jnp.einsum(
        "pcu,oue->pcoe", normed_steps_list, adapter_down_weight, preferred_element_type=jnp.float32
    )
    picked = jnp.sum(partial_down * owned.astype(jnp.float32)[None, :, :, None], axis=2)
    down_projected = lax.psum(picked, "tensor").astype(jnp.bfloat16)
    up_projected = down_projected[:, :, None, :] * owned[None, :, :, None]
    adapter_delta = jnp.einsum(
        "bcuo,uoz->bcz", up_projected, adapter_up_weight, preferred_element_type=jnp.float32
    )
    adapter_delta = lax.psum_scatter(adapter_delta, "dp", scatter_dimension=1, tiled=True)
    mixed_out = (base + adapter_delta).astype(jnp.bfloat16)
    return (mixed_out, carried)


def solution(mesh):
    placed = (
        P(("groups", "dp")),
        P(),
        P(("groups", "dp"), "tensor", None, None),
        P(None, ("groups", "dp"), "tensor"),
        P(None, ("groups", "dp"), "tensor"),
        P(None, ("groups", "dp"), "tensor"),
        P(None, ("groups", "dp"), None),
        P(None, ("groups", "dp"), None),
        P("tensor"),
        P("tensor"),
        P("tensor"),
        P("tensor", None),
        P("dp", "tensor", None),
        P("dp", None, "tensor"),
    )
    dp, tensor = mesh.shape["dp"], mesh.shape["tensor"]
    body = per_device_any
    if dp == 4 and tensor == 4:
        body = functools.partial(per_device_pairs, dp, tensor)
    return jax.shard_map(
        body,
        mesh=mesh,
        in_specs=placed,
        out_specs=(P(None, ("groups", "dp"), "tensor"), P(("groups", "dp"), "tensor", None, None)),
        check_vma=False,
    )
```
